32 devices in a mesh: groups: 2 (over x), row: 16 (over z, y, core).
Axes of the slice: x: 2, y: 2, z: 4, core: 2. Of those that a mesh axis runs over, the one named last changes fastest.
Arguments:
- design_rows: bfloat16 [1536, 2048], P('groups', 'row'), parts along dimension 0, may hold values from -6 to 6
- design_cols: bfloat16 [1536, 2048], P('groups', 'row'), parts along dimension 0, may hold values from -0.21875 to 0.21875
- noise_std: float32 [1536], P('groups'), parts along dimension 0, may hold values from 0.3 to 1
- record_noise_amplitude: float32 [32], P(('groups', 'row')), parts along dimension 0, may hold values from 0.5 to 2
- record_correlation_length: float32 [32], P(('groups', 'row')), parts along dimension 0, may hold values from 2 to 32
- arc_lengths: int32 [24], P('groups'), parts along dimension 0, may hold values from 1 to 128, 768 in all
- arc_record_index: int32 [24], P('groups'), parts along dimension 0, may hold values from 0 to 15
- block_map: int32 [32], P('groups'), parts along dimension 0, may hold values from 0 to 15, each once
Outputs:
- normal_block: float32 [4096, 2048], P(('groups', 'row')), parts along dimension 0
The draws below stay inside these ranges and needn't reach their ends.
There are 2 independent parts, one for each index of `groups`. The reference program is written for one: setup_inputs(seed, part) draws one part's arguments, and reference() takes and returns one part's arrays. A program takes and returns all parts, laid end to end along the dimension named above; each array names one. Nothing has to cross between parts.
Inputs may be any that keep to these rules, and one draw needn't show every extreme that they name: `arc_lengths`: arcs are whole runs of observations laid end to end from the first; the lengths sum to 768 and the longest has exactly 128. `block_map`: each column block number once.
All inputs are finite; a program needn't handle non-finite values.
Results may differ from the reference program's by a relative error of at most 0.0037.
Values may be sent and summed in bfloat16 or wider, within the bound.
A program may use at most 128 MiB of HBM per device.

```python
import math
import jax
import jax.numpy as jnp
import numpy as np
from jax import lax

OBS = 768
ARC_TOTAL = 12
AM = 128
CB = 128
NR = 2048
NB = 16
NC = 2048
RECORD_TOTAL = 16


def place_ends(drawn, rng, smallest, high):
    index_at = [jax.random.randint(jax.random.fold_in(rng, axis), (), 0, length) for axis, length in enumerate(drawn.shape)]
    main_axis = drawn.shape.index(max(drawn.shape))
    next_to = index_at[:main_axis] + [(index_at[main_axis] + 1) % drawn.shape[main_axis]] + index_at[main_axis + 1:]
    return drawn.at[tuple(index_at)].set(smallest).at[tuple(next_to)].set(high)


def level_of(own_key, shape, cuts, low, high):
    gain = 1.0
    for axis_at, parts in cuts:
        draws = jax.random.uniform(jax.random.fold_in(jax.random.fold_in(own_key, 6), axis_at), (parts,), jnp.float32, low / len(cuts), high / len(cuts))
        gain = gain * jnp.repeat(jnp.exp(draws), shape[axis_at] // parts).reshape((-1,) + (1,) * (len(shape) - 1 - axis_at))
    return gain


def length_profile(count, total, most, skew):
    portions = [(1 << 20) // math.isqrt(standing ** skew) + 1 for standing in range(2, count + 1)]
    rest, holding = total - most - (count - 1), [1] * (count - 1)
    while rest > 0:
        free = [i for i in range(count - 1) if holding[i] < most]
        whole, budget = sum([portions[i] for i in free]), rest
        for i in free:
            addition = min(most - holding[i], max(1, budget * portions[i] // whole), rest)
            holding[i] = holding[i] + addition
            rest = rest - addition
    return np.array([most] + holding)


def uneven_parts(key, number_of, total, bound, slope):
    if number_of == 2:
        one = jax.random.randint(key, (), max(1, total - bound), min(bound, total - 1) + 1)
        return jnp.stack([one, total - one])
    sizes = jnp.asarray(length_profile(number_of, total, bound, slope), jnp.int32)
    couples = (number_of - 1) // 2
    source_of, receiver = sizes[1:1 + 2 * couples:2], sizes[2:2 + 2 * couples:2]
    slack = jnp.minimum(source_of - 1, bound - receiver)
    moved = jax.random.randint(jax.random.fold_in(key, 1), (couples,), 0, 1 << 20) % (slack + 1)
    sizes = sizes.at[1:1 + 2 * couples:2].set(source_of - moved).at[2:2 + 2 * couples:2].set(receiver + moved)
    return sizes[jax.random.permutation(jax.random.fold_in(key, 2), number_of)]


def scatter_about(rng, dims, width, limit, split=(), held_as=jnp.bfloat16):
    result = jax.random.normal(rng, dims, jnp.float32) * width
    if len(split) > 0:
        result = level_of(rng, dims, split, -0.22, 0.18) * result
    return jnp.clip(result, min=-limit, max=limit).astype(held_as)


def setup_inputs(seed: int = 0, part: int = 0) -> dict:
    seeds = jax.random.split(jax.random.key(seed), 9)
    part_keys = jax.random.split(jax.random.fold_in(seeds[8], part), 9)
    return {
        "design_rows": scatter_about(part_keys[0], (OBS, NR), 1.0, 6.0, ((1, 16),)),
        "design_cols": scatter_about(part_keys[1], (OBS, NC), OBS ** -0.5, 0.21875, ((1, 16),)),
        "noise_std": jnp.clip(jnp.exp(jax.random.uniform(part_keys[2], (OBS,), jnp.float32, math.log(0.3), math.log(1.0))), 0.3, 1.0),
        "record_noise_amplitude": jnp.clip(jnp.exp(math.log(2.0) - 1.3862944 * jax.random.uniform(part_keys[3], (RECORD_TOTAL,), jnp.float32) ** level_of(part_keys[3], (RECORD_TOTAL,), ((0, 16),), -0.2, 0.2)), 0.5, 2.0),
        "record_correlation_length": jnp.clip(jnp.exp(math.log(32.0) - 2.7725887 * jax.random.uniform(part_keys[4], (RECORD_TOTAL,), jnp.float32) ** level_of(part_keys[4], (RECORD_TOTAL,), ((0, 16),), -0.2, 0.2)), 2.0, 32.0),
        "arc_lengths": uneven_parts(part_keys[5], ARC_TOTAL, OBS, AM, 2).astype(jnp.int32),
        "arc_record_index": place_ends(jax.random.randint(part_keys[6], (ARC_TOTAL,), 0, RECORD_TOTAL), jax.random.fold_in(part_keys[6], 1), 0, RECORD_TOTAL - 1).astype(jnp.int32),
        "block_map": jax.random.permutation(part_keys[7], NB).astype(jnp.int32),
    }


def arc_starts(arc_lengths):
    endings = jnp.cumsum(arc_lengths).astype(jnp.int32)
    return (endings - arc_lengths).astype(jnp.int32)

def whitening(starts, arc_lengths, amplitudes, correlation, noise_std):
    offsets = jnp.arange(AM, dtype=jnp.int32)
    inside = offsets[None, :] < arc_lengths[:, None]
    indices = jnp.minimum(starts[:, None] + offsets[None, :], OBS - 1).astype(jnp.int32)
    noise_level = noise_std[indices]
    observation_separation = jnp.abs(offsets[:, None] - offsets[None, :]).astype(jnp.float32)
    kernel = (amplitudes * amplitudes)[:, None, None] * jnp.exp(-observation_separation[None, :, :] / correlation[:, None, None])
    live_pair = inside[:, :, None] & inside[:, None, :]
    identity = jnp.eye(AM, dtype=jnp.float32)
    covariance = jnp.where(live_pair, kernel + identity[None, :, :] * (noise_level * noise_level)[:, :, None], identity[None, :, :])
    cholesky_factor = jnp.linalg.cholesky(covariance)
    return lax.linalg.triangular_solve(cholesky_factor, jnp.broadcast_to(identity, cholesky_factor.shape), left_side=True, lower=True)

def whiten(design, starts, arc_lengths, inverse):
    offsets = jnp.arange(AM, dtype=jnp.int32)
    inside = offsets[None, :] < arc_lengths[:, None]
    indices = jnp.minimum(starts[:, None] + offsets[None, :], OBS - 1).astype(jnp.int32)
    padded = jnp.where(inside[:, :, None], design[indices].astype(jnp.float32), jnp.float32(0.0))
    mixed = jnp.einsum('kab,kbn->kan', inverse, padded, precision=lax.Precision.HIGHEST)
    observed = jnp.arange(OBS, dtype=jnp.int32)
    arc_index = jnp.sum((starts[:, None] <= observed[None, :]).astype(jnp.int32), axis=0) - 1
    arc_place = observed - starts[arc_index]
    stacked = mixed.reshape(ARC_TOTAL * AM, design.shape[1])
    return stacked[arc_index * AM + arc_place].astype(jnp.bfloat16)

def reference(design_rows, design_cols, noise_std, record_noise_amplitude, record_correlation_length, arc_lengths, arc_record_index, block_map):
    starts = arc_starts(arc_lengths)
    inverse = whitening(starts, arc_lengths, record_noise_amplitude[arc_record_index], record_correlation_length[arc_record_index], noise_std)
    rows_white = whiten(design_rows, starts, arc_lengths, inverse)
    cols_white = whiten(design_cols, starts, arc_lengths, inverse)
    blocks = cols_white.reshape(OBS, NB, CB)[:, block_map, :].reshape(OBS, NC)
    return lax.dot_general(rows_white.astype(jnp.float32), blocks.astype(jnp.float32), (((0,), (0,)), ((), ())), preferred_element_type=jnp.float32)
```

```python
import functools

import jax
import jax.numpy as jnp
from jax import lax
from jax.experimental import pallas as pl
from jax.experimental.pallas import tpu as pltpu
from jax.sharding import PartitionSpec as P

LANES = 128
MESH = pl.DeviceIdType.MESH
F32 = jnp.float32
BF16 = jnp.bfloat16


def flat_shift(x, d):
    rolled = pltpu.roll(x, d, 1)
    above = pltpu.roll(rolled, 1, 0)
    lane = lax.broadcasted_iota(jnp.int32, x.shape, 1)
    return jnp.where(lane < d, above, rolled)


def factor_terms(lengths_ref, record_ref, recs, noise):
    shape = noise.shape
    flat = lax.broadcasted_iota(jnp.int32, shape, 0) * LANES + lax.broadcasted_iota(jnp.int32, shape, 1)
    sub = shape[0]
    start = jnp.int32(0)
    starts = jnp.zeros(shape, jnp.int32)
    amp = recs[record_ref[0], :sub]
    corr = recs[record_ref[0], sub:]
    for k in range(1, lengths_ref.shape[0]):
        start = start + lengths_ref[k - 1]
        here = flat >= start
        starts = jnp.where(here, start, starts)
        amp = jnp.where(here, recs[record_ref[k], :sub], amp)
        corr = jnp.where(here, recs[record_ref[k], sub:], corr)
    place = flat - starts
    a2 = amp * amp
    phi = jnp.exp(-1.0 / corr)
    phi2 = phi * phi
    q = a2 * (1.0 - phi2)
    r = noise * noise
    rp = flat_shift(r, 1)
    first = place == 0
    m11 = jnp.where(first, 0.0, phi2 * rp + q)
    m12 = jnp.where(first, a2, q * rp)
    m21 = jnp.where(first, 0.0, 1.0)
    m22 = jnp.where(first, 1.0, rp)
    d = 1
    while d < LANES:
        n11, n12, n21, n22 = (flat_shift(x, d) for x in (m11, m12, m21, m22))
        p11 = m11 * n11 + m12 * n21
        p12 = m11 * n12 + m12 * n22
        p21 = m21 * n11 + m22 * n21
        p22 = m21 * n12 + m22 * n22
        scale = 1.0 / (p11 + p12 + p21 + p22)
        m11, m12, m21, m22 = p11 * scale, p12 * scale, p21 * scale, p22 * scale
        d *= 2
    var = m12 / m22
    s = var + r
    inv_s = 1.0 / s
    log_g = jnp.log(phi * r * inv_s)
    total = log_g
    d = 1
    while d < LANES:
        total = total + jnp.where(place >= d, flat_shift(total, d), 0.0)
        d *= 2
    return lax.rsqrt(s), total - log_g, total, phi * var * inv_s, starts.astype(F32)


def factor_block(b, other, cols, before, gain, starts):
    sub = before.shape[0]
    a_i = cols[:, b : b + 1]
    s_i = cols[:, sub + b : sub + b + 1]
    t_i = cols[:, 2 * sub + b : 2 * sub + b + 1]
    value = -(s_i * gain[other : other + 1, :]) * jnp.exp(a_i - before[other : other + 1, :])
    live = t_i == starts[other : other + 1, :]
    if other == b:
        i = lax.broadcasted_iota(jnp.int32, (LANES, LANES), 0)
        j = lax.broadcasted_iota(jnp.int32, (LANES, LANES), 1)
        value = jnp.where(live & (j < i), value, jnp.where(i == j, s_i, 0.0))
    else:
        value = jnp.where(live, value, 0.0)
    high = value.astype(BF16)
    low = (value - high.astype(F32)).astype(BF16)
    return high, low


def kernel(
    n,
    amp_ref, corr_ref, lengths_ref, record_ref, noise_ref, rows_ref, cols_ref,
    out_ref,
    held, rows_vm, rows_t, recs, noise_vm, u_ref, lhs,
    local_sem, rec_send, rec_recv, ring_send, ring_recv, sib_send, sib_recv,
):
    me = lax.axis_index("row")
    core = me % 2
    chip = me // 2
    sibling = chip * 2 + 1 - core
    m = n // 2
    pos = jnp.where(chip % 2 == 0, chip // 2, m - 1 - chip // 2)
    obs = rows_ref.shape[0]
    half = obs // 2
    blocks = obs // LANES
    steps = m - 1
    sub = noise_vm.shape[0]

    def device(p, c):
        p = (p + 2 * m) % m
        return jnp.where(p < m // 2, 2 * p, 2 * (m - 1 - p) + 1) * 2 + c

    own_cols = pltpu.make_async_copy(cols_ref, held.at[me], local_sem.at[0])
    own_rows = pltpu.make_async_copy(rows_ref, rows_vm, local_sem.at[1])
    own_cols.start()
    own_rows.start()

    barrier = pltpu.get_barrier_semaphore()

    def greet(o, _):
        pl.semaphore_signal(barrier, inc=1, device_id={"row": (me + o) % n}, device_id_type=MESH)
        return 0

    lax.fori_loop(1, n, greet, 0)
    recs[me] = jnp.concatenate(
        [jnp.full((sub, LANES), amp_ref[0], F32), jnp.full((sub, LANES), corr_ref[0], F32)], axis=0
    )
    noise_vm[...] = jnp.ones_like(noise_vm)
    noise_vm[:blocks, :] = noise_ref[...]
    own_cols.wait()
    pl.semaphore_wait(barrier, n - 1)

    def record_copy(source, target):
        return pltpu.make_async_remote_copy(
            src_ref=recs.at[source], dst_ref=recs.at[source],
            send_sem=rec_send.at[target], recv_sem=rec_recv.at[source],
            device_id={"row": target}, device_id_type=MESH,
        )

    def send_record(o, _):
        record_copy(me, (me + o) % n).start()
        return 0

    lax.fori_loop(1, n, send_record, 0)

    def chunk_of(direction, k):
        return pl.ds(((k + direction) % 2) * half, half)

    def sign(direction):
        return 1 - 2 * direction

    def ring_copy(direction, k, at):
        origin = device(at - sign(direction) * (k // 2), core)
        part = held.at[origin, chunk_of(direction, k)]
        return pltpu.make_async_remote_copy(
            src_ref=part, dst_ref=part,
            send_sem=ring_send.at[direction, k], recv_sem=ring_recv.at[direction, k],
            device_id={"row": device(pos + sign(direction), core)}, device_id_type=MESH,
        )

    def sibling_copy(direction, k, c):
        origin = device(pos - sign(direction) * (k // 2 + 1), c)
        part = held.at[origin, chunk_of(direction, k)]
        return pltpu.make_async_remote_copy(
            src_ref=part, dst_ref=part,
            send_sem=sib_send.at[direction, k], recv_sem=sib_recv.at[direction, k],
            device_id={"row": sibling}, device_id_type=MESH,
        )

    def own_copy(c):
        part = held.at[chip * 2 + c]
        return pltpu.make_async_remote_copy(
            src_ref=part, dst_ref=part,
            send_sem=sib_send.at[0, steps], recv_sem=sib_recv.at[0, steps],
            device_id={"row": sibling}, device_id_type=MESH,
        )

    for k in range(2):
        for direction in range(2):
            ring_copy(direction, k, pos).start()
    own_copy(core).start()

    def pass_on(k, more):
        for direction in range(2):
            ring_copy(direction, k, pos - sign(direction)).wait_recv()
            if more:
                ring_copy(direction, k + 2, pos).start()
            sibling_copy(direction, k, core).start()

    def take(k):
        for direction in range(2):
            sibling_copy(direction, k, 1 - core).wait_recv()

    def tile(block):
        both = jnp.dot(lhs[...], held[block], preferred_element_type=F32)
        out_ref[block] = both[:LANES] + both[LANES:]

    own_rows.wait()
    for b in range(blocks):
        rows_t[:, b * LANES : (b + 1) * LANES] = (
            rows_vm[b * LANES : (b + 1) * LANES, :].astype(F32).T.astype(BF16)
        )

    def take_record(o, _):
        record_copy((me + o) % n, me).wait_recv()
        return 0

    lax.fori_loop(1, n, take_record, 0)
    scale, after, before, gain, starts = factor_terms(lengths_ref, record_ref, recs, noise_vm[...])
    cols = jnp.concatenate(
        [after, scale, starts, jnp.zeros((LANES - 3 * sub, LANES), F32)], axis=0
    ).T
    u_ref[...] = jnp.zeros_like(u_ref)

    def mix(b):
        near = [b] if b == 0 else [b - 1, b]
        parts = [factor_block(b, other, cols, before, gain, starts) for other in near]
        white = jnp.zeros((LANES, LANES), F32)
        for other, (high, low) in zip(near, parts):
            left = rows_t[:, other * LANES : (other + 1) * LANES]
            for term in (high, low):
                white += lax.dot_general(left, term, (((1,), (1,)), ((), ())), preferred_element_type=F32)
        white = white.astype(BF16)
        for other, (high, low) in zip(near, parts):
            u_ref[:, other * LANES : (other + 1) * LANES] += jnp.dot(
                white, high, preferred_element_type=F32
            ) + jnp.dot(white, low, preferred_element_type=F32)

    pass_on(0, steps > 2)
    for b in range(blocks // 2):
        mix(b)
    pass_on(1, steps > 3)
    for b in range(blocks // 2, blocks):
        mix(b)
    u = u_ref[...]
    high = u.astype(BF16)
    lhs[:LANES, :] = high
    lhs[LANES:, :] = (u - high.astype(F32)).astype(BF16)

    pass_on(2, steps > 4)
    own_copy(1 - core).wait_recv()
    tile(me)
    tile(sibling)

    def tiles_at(d):
        for direction in range(2):
            for c in range(2):
                tile(device(pos - sign(direction) * d, c))

    take(0)
    take(1)
    tiles_at(1)

    last = m // 2 - 1

    def one(d, odd_more, even_more):
        pass_on(2 * d - 1, odd_more)
        pass_on(2 * d, even_more)
        take(2 * d - 2)
        take(2 * d - 1)
        tiles_at(d)

    if last > 3:
        def body(d, _):
            one(d, True, True)
            return 0

        lax.fori_loop(2, last - 1, body, 0)
        first = last - 1
    else:
        first = 2
    for d in range(first, last + 1):
        one(d, 2 * d - 1 + 2 < steps, 2 * d + 2 < steps)
    take(steps - 1)
    far = device(pos + m // 2, 0)
    tile(far)
    tile(far + 1)

    def left(k, _):
        for direction in range(2):
            ring_copy(direction, k, pos).wait_send()
            sibling_copy(direction, k, core).wait_send()
        return 0

    lax.fori_loop(0, steps, left, 0)
    own_copy(core).wait_send()

    def record_left(o, _):
        record_copy(me, (me + o) % n).wait_send()
        return 0

    lax.fori_loop(1, n, record_left, 0)


def gather_multiply(n, amp, corr, lengths, record, noise, rows, cols):
    obs, width = cols.shape
    sub = -(-noise.shape[0] // 8) * 8
    steps = n // 2 - 1
    smem = pl.BlockSpec(memory_space=pltpu.SMEM)
    vmem = pl.BlockSpec(memory_space=pltpu.VMEM)
    hbm = pl.BlockSpec(memory_space=pl.ANY)
    dma = pltpu.SemaphoreType.DMA
    return pl.pallas_call(
        functools.partial(kernel, n),
        out_shape=jax.ShapeDtypeStruct((n, rows.shape[1], width), F32),
        in_specs=[smem, smem, smem, smem, vmem, hbm, hbm],
        out_specs=vmem,
        scratch_shapes=[
            pltpu.VMEM((n, obs, width), BF16),
            pltpu.VMEM((obs, LANES), BF16),
            pltpu.VMEM((LANES, obs), BF16),
            pltpu.VMEM((n, 2 * sub, LANES), F32),
            pltpu.VMEM((sub, LANES), F32),
            pltpu.VMEM((LANES, obs), F32),
            pltpu.VMEM((2 * LANES, obs), BF16),
            dma((2,)),
            dma((n,)),
            dma((n,)),
            dma((2, steps)),
            dma((2, steps)),
            dma((2, steps + 1)),
            dma((2, steps + 1)),
        ],
        compiler_params=pltpu.CompilerParams(
            collective_id=0, has_side_effects=True, vmem_limit_bytes=56 * 1024 * 1024
        ),
    )(amp, corr, lengths, record, noise, rows, cols)


def place_kernel(map_ref, tiles_ref, out_ref, sems):
    count, _, width = tiles_ref.shape

    def copy(j):
        return pltpu.make_async_copy(
            tiles_ref.at[map_ref[j]],
            out_ref.at[:, pl.ds(pl.multiple_of(j * width, width), width)],
            sems.at[j],
        )

    for j in range(count):
        copy(j).start()
    for j in range(count):
        copy(j).wait()


def place_blocks(block_map, tiles):
    count, height, width = tiles.shape
    return pl.pallas_call(
        place_kernel,
        out_shape=jax.ShapeDtypeStruct((height, count * width), F32),
        in_specs=[pl.BlockSpec(memory_space=pltpu.SMEM), pl.BlockSpec(memory_space=pl.ANY)],
        out_specs=pl.BlockSpec(memory_space=pl.ANY),
        scratch_shapes=[pltpu.SemaphoreType.DMA((count,))],
    )(block_map, tiles)


def per_device(
    design_rows,
    design_cols,
    noise_std,
    record_noise_amplitude,
    record_correlation_length,
    arc_lengths,
    arc_record_index,
    block_map,
):
    n = lax.axis_size("row")
    noise = noise_std.reshape(-1, LANES)
    tiles = gather_multiply(
        n,
        record_noise_amplitude,
        record_correlation_length,
        arc_lengths,
        arc_record_index,
        noise,
        design_rows,
        design_cols,
    )
    return place_blocks(block_map, tiles)


def solution(mesh):
    return jax.shard_map(
        per_device,
        mesh=mesh,
        in_specs=(
            P("groups", "row"),
            P("groups", "row"),
            P("groups"),
            P(("groups", "row")),
            P(("groups", "row")),
            P("groups"),
            P("groups"),
            P("groups"),
        ),
        out_specs=P(("groups", "row"), None),
        check_vma=False,
    )
```

```python
import functools

import jax
import jax.numpy as jnp
from jax import lax
from jax.experimental import pallas as pl
from jax.experimental.pallas import tpu as pltpu
from jax.sharding import PartitionSpec as P

LANES = 128
MESH = pl.DeviceIdType.MESH
F32 = jnp.float32
BF16 = jnp.bfloat16


def flat_shift(x, d):
    rolled = pltpu.roll(x, d, 1)
    above = pltpu.roll(rolled, 1, 0)
    lane = lax.broadcasted_iota(jnp.int32, x.shape, 1)
    return jnp.where(lane < d, above, rolled)


def factor_terms(lengths_ref, record_ref, recs, noise):
    shape = noise.shape
    flat = lax.broadcasted_iota(jnp.int32, shape, 0) * LANES + lax.broadcasted_iota(jnp.int32, shape, 1)
    start = jnp.int32(0)
    starts = jnp.zeros(shape, jnp.int32)
    amp = jnp.broadcast_to(recs[record_ref[0], 0:1], shape)
    corr = jnp.broadcast_to(recs[record_ref[0], 1:2], shape)
    for k in range(1, lengths_ref.shape[0]):
        start = start + lengths_ref[k - 1]
        here = flat >= start
        starts = jnp.where(here, start, starts)
        amp = jnp.where(here, recs[record_ref[k], 0:1], amp)
        corr = jnp.where(here, recs[record_ref[k], 1:2], corr)
    place = flat - starts
    a2 = amp * amp
    phi = jnp.exp(-1.0 / corr)
    phi2 = phi * phi
    q = a2 * (1.0 - phi2)
    r = noise * noise
    rp = flat_shift(r, 1)
    first = place == 0
    m11 = jnp.where(first, 0.0, phi2 * rp + q)
    m12 = jnp.where(first, a2, q * rp)
    m21 = jnp.where(first, 0.0, 1.0)
    m22 = jnp.where(first, 1.0, rp)
    d = 1
    while d < LANES:
        n11, n12, n21, n22 = (flat_shift(x, d) for x in (m11, m12, m21, m22))
        p11 = m11 * n11 + m12 * n21
        p12 = m11 * n12 + m12 * n22
        p21 = m21 * n11 + m22 * n21
        p22 = m21 * n12 + m22 * n22
        m11, m12, m21, m22 = p11, p12, p21, p22
        if d in (4, 32):
            scale = 1.0 / (p11 + p12 + p21 + p22)
            m11, m12, m21, m22 = p11 * scale, p12 * scale, p21 * scale, p22 * scale
        d *= 2
    var = m12 / m22
    s = var + r
    inv_s = 1.0 / s
    log_g = jnp.log(phi * r * inv_s)
    total = log_g
    d = 1
    while d < LANES:
        total = total + jnp.where(place >= d, flat_shift(total, d), 0.0)
        d *= 2
    return lax.rsqrt(s), total - log_g, total, phi * var * inv_s, starts.astype(F32)


def factor_block(b, other, cols, before, gain, starts):
    sub = before.shape[0]
    a_i = cols[:, b : b + 1]
    s_i = cols[:, sub + b : sub + b + 1]
    t_i = cols[:, 2 * sub + b : 2 * sub + b + 1]
    value = -(s_i * gain[other : other + 1, :]) * jnp.exp(a_i - before[other : other + 1, :])
    live = t_i == starts[other : other + 1, :]
    if other == b:
        i = lax.broadcasted_iota(jnp.int32, (LANES, LANES), 0)
        j = lax.broadcasted_iota(jnp.int32, (LANES, LANES), 1)
        value = jnp.where(live & (j < i), value, jnp.where(i == j, s_i, 0.0))
    else:
        value = jnp.where(live, value, 0.0)
    high = value.astype(BF16)
    low = (value - high.astype(F32)).astype(BF16)
    return high, low


def kernel(
    n,
    amp_ref, corr_ref, lengths_ref, record_ref, noise_ref, rows_ref, cols_ref,
    out_ref,
    held, rows_vm, rows_t, recs, noise_vm, u_ref, lhs,
    local_sem, rec_send, rec_recv, ring_send, ring_recv, sib_send, sib_recv,
):
    me = lax.axis_index("row")
    core = me % 2
    chip = me // 2
    sibling = chip * 2 + 1 - core
    m = n // 2
    pos = jnp.where(chip % 2 == 0, chip // 2, m - 1 - chip // 2)
    obs = rows_ref.shape[0]
    half = obs // 2
    blocks = obs // LANES
    steps = m - 1
    sub = noise_vm.shape[0]

    def device(p, c):
        p = (p + 2 * m) % m
        return jnp.where(p < m // 2, 2 * p, 2 * (m - 1 - p) + 1) * 2 + c

    own_cols = pltpu.make_async_copy(cols_ref, held.at[me], local_sem.at[0])
    own_rows = pltpu.make_async_copy(rows_ref, rows_vm, local_sem.at[1])
    own_cols.start()
    own_rows.start()

    barrier = pltpu.get_barrier_semaphore()

    def greet(o, _):
        pl.semaphore_signal(barrier, inc=1, device_id={"row": (me + o) % n}, device_id_type=MESH)
        return 0

    lax.fori_loop(1, n, greet, 0)
    recs[me, 0:1] = jnp.broadcast_to(amp_ref[...], (1, LANES))
    recs[me, 1:2] = jnp.broadcast_to(corr_ref[...], (1, LANES))
    noise_vm[...] = jnp.ones_like(noise_vm)
    noise_vm[:blocks, :] = noise_ref[...]
    own_rows.wait()
    for b in range(blocks):
        rows_t[:, b * LANES : (b + 1) * LANES] = (
            rows_vm[b * LANES : (b + 1) * LANES, :].astype(F32).T.astype(BF16)
        )
    own_cols.wait()
    pl.semaphore_wait(barrier, n - 1)

    def record_copy(source, target):
        return pltpu.make_async_remote_copy(
            src_ref=recs.at[source], dst_ref=recs.at[source],
            send_sem=rec_send.at[target], recv_sem=rec_recv.at[source],
            device_id={"row": target}, device_id_type=MESH,
        )

    def send_record(o, _):
        record_copy(me, (me + o) % n).start()
        return 0

    def chunk_of(direction, k):
        return pl.ds(((k + direction) % 2) * half, half)

    def sign(direction):
        return 1 - 2 * direction

    def ring_copy(direction, k, at):
        origin = device(at - sign(direction) * (k // 2), core)
        part = held.at[origin, chunk_of(direction, k)]
        return pltpu.make_async_remote_copy(
            src_ref=part, dst_ref=part,
            send_sem=ring_send.at[direction, k], recv_sem=ring_recv.at[direction, k],
            device_id={"row": device(pos + sign(direction), core)}, device_id_type=MESH,
        )

    def sibling_copy(direction, k, c):
        origin = device(pos - sign(direction) * (k // 2 + 1), c)
        part = held.at[origin, chunk_of(direction, k)]
        return pltpu.make_async_remote_copy(
            src_ref=part, dst_ref=part,
            send_sem=sib_send.at[direction, k], recv_sem=sib_recv.at[direction, k],
            device_id={"row": sibling}, device_id_type=MESH,
        )

    def own_copy(c):
        part = held.at[chip * 2 + c]
        return pltpu.make_async_remote_copy(
            src_ref=part, dst_ref=part,
            send_sem=sib_send.at[0, steps], recv_sem=sib_recv.at[0, steps],
            device_id={"row": sibling}, device_id_type=MESH,
        )

    for direction in range(2):
        ring_copy(direction, 0, pos).start()
    lax.fori_loop(1, n, send_record, 0)
    for direction in range(2):
        ring_copy(direction, 1, pos).start()
    own_copy(core).start()

    def pass_on(k, more):
        for direction in range(2):
            ring_copy(direction, k, pos - sign(direction)).wait_recv()
            if more:
                ring_copy(direction, k + 2, pos).start()
            sibling_copy(direction, k, core).start()

    def take(k):
        for direction in range(2):
            sibling_copy(direction, k, 1 - core).wait_recv()

    def tiles(p):
        block = device(p, 0)
        pair = jnp.concatenate([held[block], held[block + 1]], axis=1)
        both = jnp.dot(lhs[...], pair, preferred_element_type=F32)
        both = both[:LANES] + both[LANES:]
        out_ref[block] = both[:, :LANES]
        out_ref[block + 1] = both[:, LANES:]

    pass_on(0, steps > 2)

    def take_record(o, _):
        record_copy((me + o) % n, me).wait_recv()
        return 0

    lax.fori_loop(1, n, take_record, 0)
    scale, after, before, gain, starts = factor_terms(lengths_ref, record_ref, recs, noise_vm[...])
    cols = jnp.concatenate(
        [after, scale, starts, jnp.zeros((LANES - 3 * sub, LANES), F32)], axis=0
    ).T
    u_ref[...] = jnp.zeros_like(u_ref)

    def mix(b):
        near = [b] if b == 0 else [b - 1, b]
        parts = [factor_block(b, other, cols, before, gain, starts) for other in near]
        white = jnp.zeros((LANES, LANES), F32)
        for other, (high, low) in zip(near, parts):
            left = rows_t[:, other * LANES : (other + 1) * LANES]
            for term in (high, low):
                white += lax.dot_general(left, term, (((1,), (1,)), ((), ())), preferred_element_type=F32)
        white = white.astype(BF16)
        for other, (high, low) in zip(near, parts):
            u_ref[:, other * LANES : (other + 1) * LANES] += jnp.dot(
                white, high, preferred_element_type=F32
            ) + jnp.dot(white, low, preferred_element_type=F32)

    pass_on(1, steps > 3)
    for b in range(blocks // 2):
        mix(b)
    pass_on(2, steps > 4)
    for b in range(blocks // 2, blocks):
        mix(b)
    u = u_ref[...]
    high = u.astype(BF16)
    lhs[:LANES, :] = high
    lhs[LANES:, :] = (u - high.astype(F32)).astype(BF16)

    def tiles_at(d):
        for direction in range(2):
            tiles(pos - sign(direction) * d)

    def one(d, odd_more, even_more):
        pass_on(2 * d - 1, odd_more)
        take(2 * d - 4)
        take(2 * d - 3)
        tiles_at(d - 1)
        pass_on(2 * d, even_more)

    own_copy(1 - core).wait_recv()
    last = m // 2 - 1
    first = 2
    if last > 3:
        def body(d, _):
            one(d, True, True)
            return 0

        first = last - 1
        lax.fori_loop(2, first, body, 0)
    for d in range(first, last + 1):
        if d == first:
            tiles(pos)
        one(d, 2 * d + 1 < steps, 2 * d + 2 < steps)
    take(2 * last - 2)
    take(2 * last - 1)
    tiles_at(last)
    take(steps - 1)
    tiles(pos + m // 2)

    def left(k, _):
        for direction in range(2):
            ring_copy(direction, k, pos).wait_send()
            sibling_copy(direction, k, core).wait_send()
        return 0

    lax.fori_loop(0, steps, left, 0)
    own_copy(core).wait_send()

    def record_left(o, _):
        record_copy(me, (me + o) % n).wait_send()
        return 0

    lax.fori_loop(1, n, record_left, 0)


def gather_multiply(n, amp, corr, lengths, record, noise, rows, cols):
    obs, width = cols.shape
    sub = -(-noise.shape[0] // 8) * 8
    steps = n // 2 - 1
    smem = pl.BlockSpec(memory_space=pltpu.SMEM)
    vmem = pl.BlockSpec(memory_space=pltpu.VMEM)
    hbm = pl.BlockSpec(memory_space=pl.ANY)
    dma = pltpu.SemaphoreType.DMA
    return pl.pallas_call(
        functools.partial(kernel, n),
        out_shape=jax.ShapeDtypeStruct((n, rows.shape[1], width), F32),
        in_specs=[vmem, vmem, smem, smem, vmem, hbm, hbm],
        out_specs=vmem,
        scratch_shapes=[
            pltpu.VMEM((n, obs, width), BF16),
            pltpu.VMEM((obs, LANES), BF16),
            pltpu.VMEM((LANES, obs), BF16),
            pltpu.VMEM((n, 8, LANES), F32),
            pltpu.VMEM((sub, LANES), F32),
            pltpu.VMEM((LANES, obs), F32),
            pltpu.VMEM((2 * LANES, obs), BF16),
            dma((2,)),
            dma((n,)),
            dma((n,)),
            dma((2, steps)),
            dma((2, steps)),
            dma((2, steps + 1)),
            dma((2, steps + 1)),
        ],
        compiler_params=pltpu.CompilerParams(
            collective_id=0, has_side_effects=True, vmem_limit_bytes=56 * 1024 * 1024
        ),
    )(amp, corr, lengths, record, noise, rows, cols)


def place_kernel(map_ref, tiles_ref, out_ref, row, in_sem, out_sem):
    count, _, width = tiles_ref.shape

    def columns(j):
        return pl.ds(j * width, width)

    def bring(j):
        return pltpu.make_async_copy(tiles_ref.at[map_ref[j]], row.at[:, columns(j)], in_sem.at[j])

    def put(j):
        return pltpu.make_async_copy(row.at[:, columns(j)], out_ref.at[:, columns(j)], out_sem.at[j])

    for j in range(count):
        bring(j).start()
    for j in range(count):
        bring(j).wait()
        put(j).start()
    for j in range(count):
        put(j).wait()


def place_blocks(block_map, tiles):
    count, height, width = tiles.shape
    return pl.pallas_call(
        place_kernel,
        out_shape=jax.ShapeDtypeStruct((height, count * width), F32),
        in_specs=[pl.BlockSpec(memory_space=pltpu.SMEM), pl.BlockSpec(memory_space=pl.ANY)],
        out_specs=pl.BlockSpec(memory_space=pl.ANY),
        scratch_shapes=[
            pltpu.VMEM((height, count * width), F32),
            pltpu.SemaphoreType.DMA((count,)),
            pltpu.SemaphoreType.DMA((count,)),
        ],
        compiler_params=pltpu.CompilerParams(vmem_limit_bytes=56 * 1024 * 1024),
    )(block_map, tiles)


def per_device(
    design_rows,
    design_cols,
    noise_std,
    record_noise_amplitude,
    record_correlation_length,
    arc_lengths,
    arc_record_index,
    block_map,
):
    n = lax.axis_size("row")
    noise = noise_std.reshape(-1, LANES)
    tiles = gather_multiply(
        n,
        record_noise_amplitude.reshape(1, 1),
        record_correlation_length.reshape(1, 1),
        arc_lengths,
        arc_record_index,
        noise,
        design_rows,
        design_cols,
    )
    return place_blocks(block_map, tiles)


def solution(mesh):
    return jax.shard_map(
        per_device,
        mesh=mesh,
        in_specs=(
            P("groups", "row"),
            P("groups", "row"),
            P("groups"),
            P(("groups", "row")),
            P(("groups", "row")),
            P("groups"),
            P("groups"),
            P("groups"),
        ),
        out_specs=P(("groups", "row"), None),
        check_vma=False,
    )
```

```python
import functools

import jax
import jax.numpy as jnp
from jax import lax
from jax.experimental import pallas as pl
from jax.experimental.pallas import tpu as pltpu
from jax.sharding import PartitionSpec as P

LANES = 128
MESH = pl.DeviceIdType.MESH
F32 = jnp.float32
BF16 = jnp.bfloat16


def flat_shift(x, d):
    rolled = pltpu.roll(x, d, 1)
    above = pltpu.roll(rolled, 1, 0)
    lane = lax.broadcasted_iota(jnp.int32, x.shape, 1)
    return jnp.where(lane < d, above, rolled)


def record_terms(lengths_ref, record_ref, recs, shape):
    flat = lax.broadcasted_iota(jnp.int32, shape, 0) * LANES + lax.broadcasted_iota(jnp.int32, shape, 1)
    start = jnp.int32(0)
    starts = jnp.zeros(shape, jnp.int32)
    amp = jnp.broadcast_to(recs[record_ref[0], 0:1], shape)
    corr = jnp.broadcast_to(recs[record_ref[0], 1:2], shape)
    for k in range(1, lengths_ref.shape[0]):
        start = start + lengths_ref[k - 1]
        here = flat >= start
        starts = jnp.where(here, start, starts)
        amp = jnp.where(here, recs[record_ref[k], 0:1], amp)
        corr = jnp.where(here, recs[record_ref[k], 1:2], corr)
    return amp, corr, starts.astype(F32), flat - starts


def filter_terms(amp, corr, place, noise):
    a2 = amp * amp
    phi = jnp.exp(-1.0 / corr)
    phi2 = phi * phi
    q = a2 * (1.0 - phi2)
    r = noise * noise
    rp = flat_shift(r, 1)
    first = place == 0
    m11 = jnp.where(first, 0.0, phi2 * rp + q)
    m12 = jnp.where(first, a2, q * rp)
    m21 = jnp.where(first, 0.0, 1.0)
    m22 = jnp.where(first, 1.0, rp)
    d = 1
    while d < LANES:
        n11, n12, n21, n22 = (flat_shift(x, d) for x in (m11, m12, m21, m22))
        p11 = m11 * n11 + m12 * n21
        p12 = m11 * n12 + m12 * n22
        p21 = m21 * n11 + m22 * n21
        p22 = m21 * n12 + m22 * n22
        m11, m12, m21, m22 = p11, p12, p21, p22
        if d in (4, 32):
            scale = 1.0 / (p11 + p12 + p21 + p22)
            m11, m12, m21, m22 = p11 * scale, p12 * scale, p21 * scale, p22 * scale
        d *= 2
    var = m12 / m22
    s = var + r
    inv_s = 1.0 / s
    return lax.rsqrt(s), jnp.log(phi * r * inv_s), phi * var * inv_s


def log_sums(log_g, place):
    total = log_g
    d = 1
    while d < LANES:
        total = total + jnp.where(place >= d, flat_shift(total, d), 0.0)
        d *= 2
    return total - log_g, total


def factor_block(b, other, cols, before, gain, starts):
    sub = before.shape[0]
    a_i = cols[:, b : b + 1]
    s_i = cols[:, sub + b : sub + b + 1]
    t_i = cols[:, 2 * sub + b : 2 * sub + b + 1]
    value = -(s_i * gain[other : other + 1, :]) * jnp.exp(a_i - before[other : other + 1, :])
    live = t_i == starts[other : other + 1, :]
    if other == b:
        i = lax.broadcasted_iota(jnp.int32, (LANES, LANES), 0)
        j = lax.broadcasted_iota(jnp.int32, (LANES, LANES), 1)
        value = jnp.where(live & (j < i), value, jnp.where(i == j, s_i, 0.0))
    else:
        value = jnp.where(live, value, 0.0)
    high = value.astype(BF16)
    low = (value - high.astype(F32)).astype(BF16)
    return high, low


def kernel(
    n,
    amp_ref, corr_ref, lengths_ref, record_ref, noise_ref, rows_ref, cols_ref,
    out_ref,
    held, rows_vm, rows_t, recs, noise_vm, u_ref, lhs,
    local_sem, rec_send, rec_recv, ring_send, ring_recv, sib_send, sib_recv,
):
    me = lax.axis_index("row")
    core = me % 2
    chip = me // 2
    sibling = chip * 2 + 1 - core
    m = n // 2
    pos = jnp.where(chip % 2 == 0, chip // 2, m - 1 - chip // 2)
    obs = rows_ref.shape[0]
    half = obs // 2
    blocks = obs // LANES
    steps = m - 1
    sub = noise_vm.shape[0]

    def device(p, c):
        p = (p + 2 * m) % m
        return jnp.where(p < m // 2, 2 * p, 2 * (m - 1 - p) + 1) * 2 + c

    own_cols = pltpu.make_async_copy(cols_ref, held.at[me], local_sem.at[0])
    own_rows = pltpu.make_async_copy(rows_ref, rows_vm, local_sem.at[1])
    own_cols.start()
    own_rows.start()

    barrier = pltpu.get_barrier_semaphore()

    def greet(o, _):
        pl.semaphore_signal(barrier, inc=1, device_id={"row": (me + o) % n}, device_id_type=MESH)
        return 0

    lax.fori_loop(1, n, greet, 0)
    recs[me, 0:1] = jnp.broadcast_to(amp_ref[...], (1, LANES))
    recs[me, 1:2] = jnp.broadcast_to(corr_ref[...], (1, LANES))
    noise_vm[...] = jnp.ones_like(noise_vm)
    noise_vm[:blocks, :] = noise_ref[...]
    own_rows.wait()
    for b in range(blocks):
        rows_t[:, b * LANES : (b + 1) * LANES] = (
            rows_vm[b * LANES : (b + 1) * LANES, :].astype(F32).T.astype(BF16)
        )
    own_cols.wait()
    pl.semaphore_wait(barrier, n - 1)

    def record_copy(source, target):
        return pltpu.make_async_remote_copy(
            src_ref=recs.at[source], dst_ref=recs.at[source],
            send_sem=rec_send.at[target], recv_sem=rec_recv.at[source],
            device_id={"row": target}, device_id_type=MESH,
        )

    def send_record(o, _):
        record_copy(me, (me + o) % n).start()
        return 0

    def half_of(direction, h):
        return ((h + direction) % 2) * half

    def sign(direction):
        return 1 - 2 * direction

    def ring_copy(direction, h, q, at):
        origin = device(at - sign(direction) * (h // 2), core)
        part = held.at[origin, pl.ds(half_of(direction, h) + q * (half // 2), half // 2)]
        return pltpu.make_async_remote_copy(
            src_ref=part, dst_ref=part,
            send_sem=ring_send.at[direction, 2 * h + q], recv_sem=ring_recv.at[direction, 2 * h + q],
            device_id={"row": device(pos + sign(direction), core)}, device_id_type=MESH,
        )

    def sibling_copy(direction, h, c):
        origin = device(pos - sign(direction) * (h // 2 + 1), c)
        part = held.at[origin, pl.ds(half_of(direction, h), half)]
        return pltpu.make_async_remote_copy(
            src_ref=part, dst_ref=part,
            send_sem=sib_send.at[direction, h], recv_sem=sib_recv.at[direction, h],
            device_id={"row": sibling}, device_id_type=MESH,
        )

    def own_copy(c):
        part = held.at[chip * 2 + c]
        return pltpu.make_async_remote_copy(
            src_ref=part, dst_ref=part,
            send_sem=sib_send.at[0, steps], recv_sem=sib_recv.at[0, steps],
            device_id={"row": sibling}, device_id_type=MESH,
        )

    for direction in range(2):
        ring_copy(direction, 0, 0, pos).start()
    lax.fori_loop(1, n, send_record, 0)
    for h, q in ((0, 1), (1, 0), (1, 1)):
        for direction in range(2):
            ring_copy(direction, h, q, pos).start()
    own_copy(core).start()

    def pass_on(h, q, more=None):
        more = h + 2 < steps if more is None else more
        for direction in range(2):
            ring_copy(direction, h, q, pos - sign(direction)).wait_recv()
            if more:
                ring_copy(direction, h + 2, q, pos).start()
            if q == 1:
                sibling_copy(direction, h, core).start()

    def take(k):
        for direction in range(2):
            sibling_copy(direction, k, 1 - core).wait_recv()

    def tiles(p):
        block = device(p, 0)
        pair = jnp.concatenate([held[block], held[block + 1]], axis=1)
        both = jnp.dot(lhs[...], pair, preferred_element_type=F32)
        both = both[:LANES] + both[LANES:]
        out_ref[block] = both[:, :LANES]
        out_ref[block + 1] = both[:, LANES:]

    u_ref[...] = jnp.zeros_like(u_ref)
    pass_on(0, 0)

    def take_record(o, _):
        record_copy((me + o) % n, me).wait_recv()
        return 0

    lax.fori_loop(1, n, take_record, 0)
    amp, corr, starts, place = record_terms(lengths_ref, record_ref, recs, noise_vm.shape)
    scale, log_g, gain = filter_terms(amp, corr, place, noise_vm[...])
    pass_on(0, 1)
    after, before = log_sums(log_g, place)
    cols = jnp.concatenate(
        [after, scale, starts, jnp.zeros((LANES - 3 * sub, LANES), F32)], axis=0
    ).T

    def mix(b):
        near = [b] if b == 0 else [b - 1, b]
        span = slice(near[0] * LANES, (b + 1) * LANES)
        wide = len(near) * LANES
        parts = [factor_block(b, other, cols, before, gain, starts) for other in near]
        both = jnp.concatenate([part[0] for part in parts] + [part[1] for part in parts], axis=1)
        left = rows_t[:, span]
        white = lax.dot_general(
            jnp.concatenate([left, left], axis=1), both, (((1,), (1,)), ((), ())), preferred_element_type=F32
        ).astype(BF16)
        back = jnp.dot(white, both, preferred_element_type=F32)
        u_ref[:, span] += back[:, :wide] + back[:, wide:]

    def tiles_at(d, direction):
        tiles(pos - sign(direction) * d)

    last = m // 2 - 1
    pass_on(1, 0)
    mix(0)
    mix(1)
    pass_on(1, 1)
    mix(2)
    mix(3)
    pass_on(2, 0)
    for b in range(4, blocks):
        mix(b)
    pass_on(2, 1)
    u = u_ref[...]
    high = u.astype(BF16)
    lhs[:LANES, :] = high
    lhs[LANES:, :] = (u - high.astype(F32)).astype(BF16)
    own_copy(1 - core).wait_recv()
    tiles(pos)
    pass_on(3, 0)
    take(0)
    take(1)
    tiles_at(1, 0)
    pass_on(3, 1)
    tiles_at(1, 1)

    def one(d, more):
        h = 2 * d - 2
        pass_on(h, 0, more)
        take(h - 2)
        take(h - 1)
        tiles_at(d - 1, 0)
        pass_on(h, 1, more)
        tiles_at(d - 1, 1)
        pass_on(h + 1, 0, more)
        pass_on(h + 1, 1, more)

    if last > 3:
        def body(d, _):
            one(d, True)
            return 0

        lax.fori_loop(3, last, body, 0)
    one(last, None)
    pass_on(steps - 1, 0)
    take(steps - 3)
    take(steps - 2)
    tiles_at(last, 0)
    pass_on(steps - 1, 1)
    tiles_at(last, 1)
    take(steps - 1)
    tiles(pos + m // 2)

    def left(k, _):
        for direction in range(2):
            for q in range(2):
                ring_copy(direction, k, q, pos).wait_send()
            sibling_copy(direction, k, core).wait_send()
        return 0

    lax.fori_loop(0, steps, left, 0)
    own_copy(core).wait_send()

    def record_left(o, _):
        record_copy(me, (me + o) % n).wait_send()
        return 0

    lax.fori_loop(1, n, record_left, 0)


def gather_multiply(n, amp, corr, lengths, record, noise, rows, cols):
    obs, width = cols.shape
    sub = -(-noise.shape[0] // 8) * 8
    steps = n // 2 - 1
    held_bytes = n * obs * width * 2
    smem = pl.BlockSpec(memory_space=pltpu.SMEM)
    vmem = pl.BlockSpec(memory_space=pltpu.VMEM)
    hbm = pl.BlockSpec(memory_space=pltpu.HBM)
    dma = pltpu.SemaphoreType.DMA
    return pl.pallas_call(
        functools.partial(kernel, n),
        out_shape=pltpu.VMEM((n, rows.shape[1], width), F32),
        in_specs=[vmem, vmem, smem, smem, vmem, hbm, hbm],
        out_specs=vmem,
        scratch_shapes=[
            pltpu.VMEM((n, obs, width), BF16),
            pltpu.VMEM((obs, LANES), BF16),
            pltpu.VMEM((LANES, obs), BF16),
            pltpu.VMEM((n, 8, LANES), F32),
            pltpu.VMEM((sub, LANES), F32),
            pltpu.VMEM((LANES, obs), F32),
            pltpu.VMEM((2 * LANES, obs), BF16),
            dma((2,)),
            dma((n,)),
            dma((n,)),
            dma((2, 2 * steps)),
            dma((2, 2 * steps)),
            dma((2, steps + 1)),
            dma((2, steps + 1)),
        ],
        compiler_params=pltpu.CompilerParams(
            collective_id=0, has_side_effects=True, vmem_limit_bytes=held_bytes + 12 * 1024 * 1024
        ),
    )(amp, corr, lengths, record, noise, rows, cols)


def place_kernel(map_ref, tiles_ref, out_ref, sems):
    count, _, width = tiles_ref.shape

    def put(j):
        return pltpu.make_async_copy(
            tiles_ref.at[map_ref[j]], out_ref.at[:, pl.ds(j * width, width)], sems.at[j]
        )

    for j in range(count):
        put(j).start()
    for j in range(count):
        put(j).wait()


def place_blocks(block_map, tiles):
    count, height, width = tiles.shape
    return pl.pallas_call(
        place_kernel,
        out_shape=jax.ShapeDtypeStruct((height, count * width), F32),
        in_specs=[pl.BlockSpec(memory_space=pltpu.SMEM), pl.BlockSpec(memory_space=pltpu.VMEM)],
        out_specs=pl.BlockSpec(memory_space=pl.ANY),
        scratch_shapes=[pltpu.SemaphoreType.DMA((count,))],
        compiler_params=pltpu.CompilerParams(vmem_limit_bytes=16 * 1024 * 1024),
    )(block_map, tiles)


def per_device(
    design_rows,
    design_cols,
    noise_std,
    record_noise_amplitude,
    record_correlation_length,
    arc_lengths,
    arc_record_index,
    block_map,
):
    n = lax.axis_size("row")
    noise = noise_std.reshape(-1, LANES)
    tiles = gather_multiply(
        n,
        record_noise_amplitude.reshape(1, 1),
        record_correlation_length.reshape(1, 1),
        arc_lengths,
        arc_record_index,
        noise,
        design_rows,
        design_cols,
    )
    return place_blocks(block_map, tiles)


def solution(mesh):
    return jax.shard_map(
        per_device,
        mesh=mesh,
        in_specs=(
            P("groups", "row"),
            P("groups", "row"),
            P("groups"),
            P(("groups", "row")),
            P(("groups", "row")),
            P("groups"),
            P("groups"),
            P("groups"),
        ),
        out_specs=P(("groups", "row"), None),
        check_vma=False,
    )
```

```python
import functools

import jax
import jax.numpy as jnp
from jax import lax
from jax.experimental import pallas as pl
from jax.experimental.pallas import tpu as pltpu
from jax.sharding import PartitionSpec as P

LANES = 128
MESH = pl.DeviceIdType.MESH
F32 = jnp.float32
BF16 = jnp.bfloat16


def flat_shift(x, d):
    rolled = pltpu.roll(x, d, 1)
    above = pltpu.roll(rolled, 1, 0)
    lane = lax.broadcasted_iota(jnp.int32, x.shape, 1)
    return jnp.where(lane < d, above, rolled)


def record_terms(lengths_ref, record_ref, recs, shape):
    flat = lax.broadcasted_iota(jnp.int32, shape, 0) * LANES + lax.broadcasted_iota(jnp.int32, shape, 1)
    start = jnp.int32(0)
    starts = jnp.zeros(shape, jnp.int32)
    amp = jnp.broadcast_to(recs[record_ref[0], 0:1], shape)
    corr = jnp.broadcast_to(recs[record_ref[0], 1:2], shape)
    for k in range(1, lengths_ref.shape[0]):
        start = start + lengths_ref[k - 1]
        here = flat >= start
        starts = jnp.where(here, start, starts)
        amp = jnp.where(here, recs[record_ref[k], 0:1], amp)
        corr = jnp.where(here, recs[record_ref[k], 1:2], corr)
    return amp, corr, starts.astype(F32), flat - starts


def filter_terms(amp, corr, place, noise):
    a2 = amp * amp
    phi = jnp.exp(-1.0 / corr)
    phi2 = phi * phi
    q = a2 * (1.0 - phi2)
    r = noise * noise
    rp = flat_shift(r, 1)
    first = place == 0
    m11 = jnp.where(first, 0.0, phi2 * rp + q)
    m12 = jnp.where(first, a2, q * rp)
    m21 = jnp.where(first, 0.0, 1.0)
    m22 = jnp.where(first, 1.0, rp)
    d = 1
    while d < LANES:
        n11, n12, n21, n22 = (flat_shift(x, d) for x in (m11, m12, m21, m22))
        p11 = m11 * n11 + m12 * n21
        p12 = m11 * n12 + m12 * n22
        p21 = m21 * n11 + m22 * n21
        p22 = m21 * n12 + m22 * n22
        m11, m12, m21, m22 = p11, p12, p21, p22
        if d in (4, 32):
            scale = 1.0 / (p11 + p12 + p21 + p22)
            m11, m12, m21, m22 = p11 * scale, p12 * scale, p21 * scale, p22 * scale
        d *= 2
    var = m12 / m22
    s = var + r
    inv_s = 1.0 / s
    return lax.rsqrt(s), jnp.log(phi * r * inv_s), phi * var * inv_s


def log_sums(log_g, place):
    total = log_g
    d = 1
    while d < LANES:
        total = total + jnp.where(place >= d, flat_shift(total, d), 0.0)
        d *= 2
    return total - log_g, total


def factor_block(b, other, cols, before, gain, starts):
    sub = before.shape[0]
    a_i = cols[:, b : b + 1]
    s_i = cols[:, sub + b : sub + b + 1]
    t_i = cols[:, 2 * sub + b : 2 * sub + b + 1]
    value = -(s_i * gain[other : other + 1, :]) * jnp.exp(a_i - before[other : other + 1, :])
    live = t_i == starts[other : other + 1, :]
    if other == b:
        i = lax.broadcasted_iota(jnp.int32, (LANES, LANES), 0)
        j = lax.broadcasted_iota(jnp.int32, (LANES, LANES), 1)
        value = jnp.where(live & (j < i), value, jnp.where(i == j, s_i, 0.0))
    else:
        value = jnp.where(live, value, 0.0)
    high = value.astype(BF16)
    low = (value - high.astype(F32)).astype(BF16)
    return high, low


def kernel(
    n,
    amp_ref, corr_ref, lengths_ref, record_ref, noise_ref, rows_ref, cols_ref,
    out_ref,
    amp_sm, corr_sm, held, rows_vm, rows_t, recs, noise_vm, u_ref, lhs,
    local_sem, rec_send, rec_recv, ring_send, ring_recv, sib_send, sib_recv,
):
    me = lax.axis_index("row")
    core = me % 2
    chip = me // 2
    sibling = chip * 2 + 1 - core
    m = n // 2
    pos = jnp.where(chip % 2 == 0, chip // 2, m - 1 - chip // 2)
    obs = rows_ref.shape[0]
    half = obs // 2
    blocks = obs // LANES
    steps = m - 1
    sub = noise_vm.shape[0]

    def device(p, c):
        p = (p + 2 * m) % m
        return jnp.where(p < m // 2, 2 * p, 2 * (m - 1 - p) + 1) * 2 + c

    own_cols = pltpu.make_async_copy(cols_ref, held.at[me], local_sem.at[0])
    own_rows = pltpu.make_async_copy(rows_ref, rows_vm, local_sem.at[1])
    own_amp = pltpu.make_async_copy(amp_ref, amp_sm, local_sem.at[2])
    own_corr = pltpu.make_async_copy(corr_ref, corr_sm, local_sem.at[3])
    own_amp.start()
    own_corr.start()
    own_cols.start()
    own_rows.start()

    barrier = pltpu.get_barrier_semaphore()

    def greet(o, _):
        pl.semaphore_signal(barrier, inc=1, device_id={"row": (me + o) % n}, device_id_type=MESH)
        return 0

    lax.fori_loop(1, n, greet, 0)
    own_amp.wait()
    own_corr.wait()
    recs[me, 0:1] = jnp.full((1, LANES), amp_sm[0], F32)
    recs[me, 1:2] = jnp.full((1, LANES), corr_sm[0], F32)
    noise_vm[...] = jnp.ones_like(noise_vm)
    noise_vm[:blocks, :] = noise_ref[...]
    own_rows.wait()
    for b in range(blocks):
        rows_t[:, b * LANES : (b + 1) * LANES] = (
            rows_vm[b * LANES : (b + 1) * LANES, :].astype(F32).T.astype(BF16)
        )
    own_cols.wait()
    pl.semaphore_wait(barrier, n - 1)

    def record_copy(source, target):
        return pltpu.make_async_remote_copy(
            src_ref=recs.at[source], dst_ref=recs.at[source],
            send_sem=rec_send.at[target], recv_sem=rec_recv.at[source],
            device_id={"row": target}, device_id_type=MESH,
        )

    def send_record(o, _):
        record_copy(me, (me + o) % n).start()
        return 0

    def half_of(direction, h):
        return ((h + direction) % 2) * half

    def sign(direction):
        return 1 - 2 * direction

    def ring_copy(direction, h, q, at):
        origin = device(at - sign(direction) * (h // 2), core)
        part = held.at[origin, pl.ds(half_of(direction, h) + q * (half // 2), half // 2)]
        return pltpu.make_async_remote_copy(
            src_ref=part, dst_ref=part,
            send_sem=ring_send.at[direction, 2 * h + q], recv_sem=ring_recv.at[direction, 2 * h + q],
            device_id={"row": device(pos + sign(direction), core)}, device_id_type=MESH,
        )

    def sibling_copy(direction, h, c):
        origin = device(pos - sign(direction) * (h // 2 + 1), c)
        part = held.at[origin, pl.ds(half_of(direction, h), half)]
        return pltpu.make_async_remote_copy(
            src_ref=part, dst_ref=part,
            send_sem=sib_send.at[direction, h], recv_sem=sib_recv.at[direction, h],
            device_id={"row": sibling}, device_id_type=MESH,
        )

    def own_copy(c):
        part = held.at[chip * 2 + c]
        return pltpu.make_async_remote_copy(
            src_ref=part, dst_ref=part,
            send_sem=sib_send.at[0, steps], recv_sem=sib_recv.at[0, steps],
            device_id={"row": sibling}, device_id_type=MESH,
        )

    for direction in range(2):
        ring_copy(direction, 0, 0, pos).start()
    lax.fori_loop(1, n, send_record, 0)
    for h, q in ((0, 1), (1, 0), (1, 1)):
        for direction in range(2):
            ring_copy(direction, h, q, pos).start()
    own_copy(core).start()

    def pass_on(h, q, more=None):
        more = h + 2 < steps if more is None else more
        for direction in range(2):
            ring_copy(direction, h, q, pos - sign(direction)).wait_recv()
            if more:
                ring_copy(direction, h + 2, q, pos).start()
            if q == 1:
                sibling_copy(direction, h, core).start()

    def take(k):
        for direction in range(2):
            sibling_copy(direction, k, 1 - core).wait_recv()

    def tiles(p):
        block = device(p, 0)
        pair = jnp.concatenate([held[block], held[block + 1]], axis=1)
        both = jnp.dot(lhs[...], pair, preferred_element_type=F32)
        both = both[:LANES] + both[LANES:]
        out_ref[block] = both[:, :LANES]
        out_ref[block + 1] = both[:, LANES:]

    u_ref[...] = jnp.zeros_like(u_ref)
    pass_on(0, 0)

    def take_record(o, _):
        record_copy((me + o) % n, me).wait_recv()
        return 0

    lax.fori_loop(1, n, take_record, 0)
    amp, corr, starts, place = record_terms(lengths_ref, record_ref, recs, noise_vm.shape)
    scale, log_g, gain = filter_terms(amp, corr, place, noise_vm[...])
    pass_on(0, 1)
    after, before = log_sums(log_g, place)
    cols = jnp.concatenate(
        [after, scale, starts, jnp.zeros((LANES - 3 * sub, LANES), F32)], axis=0
    ).T

    def mix(b):
        near = [b] if b == 0 else [b - 1, b]
        span = slice(near[0] * LANES, (b + 1) * LANES)
        wide = len(near) * LANES
        parts = [factor_block(b, other, cols, before, gain, starts) for other in near]
        both = jnp.concatenate([part[0] for part in parts] + [part[1] for part in parts], axis=1)
        left = rows_t[:, span]
        white = lax.dot_general(
            jnp.concatenate([left, left], axis=1), both, (((1,), (1,)), ((), ())), preferred_element_type=F32
        ).astype(BF16)
        back = jnp.dot(white, both, preferred_element_type=F32)
        u_ref[:, span] += back[:, :wide] + back[:, wide:]

    def tiles_at(d, direction):
        tiles(pos - sign(direction) * d)

    last = m // 2 - 1
    pass_on(1, 0)
    mix(0)
    mix(1)
    pass_on(1, 1)
    mix(2)
    mix(3)
    pass_on(2, 0)
    for b in range(4, blocks):
        mix(b)
    pass_on(2, 1)
    u = u_ref[...]
    high = u.astype(BF16)
    lhs[:LANES, :] = high
    lhs[LANES:, :] = (u - high.astype(F32)).astype(BF16)
    own_copy(1 - core).wait_recv()
    tiles(pos)
    pass_on(3, 0)
    take(0)
    take(1)
    tiles_at(1, 0)
    pass_on(3, 1)
    tiles_at(1, 1)

    def one(d, more):
        h = 2 * d - 2
        pass_on(h, 0, more)
        take(h - 2)
        take(h - 1)
        tiles_at(d - 1, 0)
        pass_on(h, 1, more)
        tiles_at(d - 1, 1)
        pass_on(h + 1, 0, more)
        pass_on(h + 1, 1, more)

    if last > 3:
        def body(d, _):
            one(d, True)
            return 0

        lax.fori_loop(3, last, body, 0)
    one(last, None)
    pass_on(steps - 1, 0)
    take(steps - 3)
    take(steps - 2)
    tiles_at(last, 0)
    pass_on(steps - 1, 1)
    tiles_at(last, 1)
    take(steps - 1)
    tiles(pos + m // 2)

    def left(k, _):
        for direction in range(2):
            for q in range(2):
                ring_copy(direction, k, q, pos).wait_send()
            sibling_copy(direction, k, core).wait_send()
        return 0

    lax.fori_loop(0, steps, left, 0)
    own_copy(core).wait_send()

    def record_left(o, _):
        record_copy(me, (me + o) % n).wait_send()
        return 0

    lax.fori_loop(1, n, record_left, 0)


def gather_multiply(n, amp, corr, lengths, record, noise, rows, cols):
    obs, width = cols.shape
    sub = -(-noise.shape[0] // 8) * 8
    steps = n // 2 - 1
    smem = pl.BlockSpec(memory_space=pltpu.SMEM)
    vmem = pl.BlockSpec(memory_space=pltpu.VMEM)
    hbm = pl.BlockSpec(memory_space=pltpu.HBM)
    dma = pltpu.SemaphoreType.DMA
    return pl.pallas_call(
        functools.partial(kernel, n),
        out_shape=pltpu.VMEM((n, rows.shape[1], width), F32),
        in_specs=[hbm, hbm, smem, smem, vmem, hbm, hbm],
        out_specs=vmem,
        scratch_shapes=[
            pltpu.SMEM((1,), F32),
            pltpu.SMEM((1,), F32),
            pltpu.VMEM((n, obs, width), BF16),
            pltpu.VMEM((obs, LANES), BF16),
            pltpu.VMEM((LANES, obs), BF16),
            pltpu.VMEM((n, 8, LANES), F32),
            pltpu.VMEM((sub, LANES), F32),
            pltpu.VMEM((LANES, obs), F32),
            pltpu.VMEM((2 * LANES, obs), BF16),
            dma((4,)),
            dma((n,)),
            dma((n,)),
            dma((2, 2 * steps)),
            dma((2, 2 * steps)),
            dma((2, steps + 1)),
            dma((2, steps + 1)),
        ],
        compiler_params=pltpu.CompilerParams(
            collective_id=0, has_side_effects=True, vmem_limit_bytes=54 * 1024 * 1024
        ),
    )(amp, corr, lengths, record, noise, rows, cols)


def place_kernel(map_ref, tiles_ref, out_ref, sems):
    count, _, width = tiles_ref.shape

    def put(j):
        return pltpu.make_async_copy(
            tiles_ref.at[map_ref[j]], out_ref.at[:, pl.ds(j * width, width)], sems.at[j]
        )

    for j in range(count):
        put(j).start()
    for j in range(count):
        put(j).wait()


def place_blocks(block_map, tiles):
    count, height, width = tiles.shape
    return pl.pallas_call(
        place_kernel,
        out_shape=jax.ShapeDtypeStruct((height, count * width), F32),
        in_specs=[pl.BlockSpec(memory_space=pltpu.SMEM), pl.BlockSpec(memory_space=pltpu.VMEM)],
        out_specs=pl.BlockSpec(memory_space=pl.ANY),
        scratch_shapes=[pltpu.SemaphoreType.DMA((count,))],
        compiler_params=pltpu.CompilerParams(vmem_limit_bytes=16 * 1024 * 1024),
    )(block_map, tiles)


def per_device(
    design_rows,
    design_cols,
    noise_std,
    record_noise_amplitude,
    record_correlation_length,
    arc_lengths,
    arc_record_index,
    block_map,
):
    n = lax.axis_size("row")
    noise = noise_std.reshape(-1, LANES)
    tiles = gather_multiply(
        n,
        record_noise_amplitude,
        record_correlation_length,
        arc_lengths,
        arc_record_index,
        noise,
        design_rows,
        design_cols,
    )
    return place_blocks(block_map, tiles)


def solution(mesh):
    return jax.shard_map(
        per_device,
        mesh=mesh,
        in_specs=(
            P("groups", "row"),
            P("groups", "row"),
            P("groups"),
            P(("groups", "row")),
            P(("groups", "row")),
            P("groups"),
            P("groups"),
            P("groups"),
        ),
        out_specs=P(("groups", "row"), None),
        check_vma=False,
    )
```

```python
import functools

import jax
import jax.numpy as jnp
from jax import lax
from jax.experimental import pallas as pl
from jax.experimental.pallas import tpu as pltpu
from jax.sharding import PartitionSpec as P

LANES = 128
MESH = pl.DeviceIdType.MESH
F32 = jnp.float32
BF16 = jnp.bfloat16


def flat_shift(x, d):
    rolled = pltpu.roll(x, d, 1)
    above = pltpu.roll(rolled, 1, 0)
    lane = lax.broadcasted_iota(jnp.int32, x.shape, 1)
    return jnp.where(lane < d, above, rolled)


def record_terms(lengths_ref, record_ref, recs, shape):
    flat = lax.broadcasted_iota(jnp.int32, shape, 0) * LANES + lax.broadcasted_iota(jnp.int32, shape, 1)
    start = jnp.int32(0)
    starts = jnp.zeros(shape, jnp.int32)
    amp = jnp.broadcast_to(recs[record_ref[0], 0:1], shape)
    corr = jnp.broadcast_to(recs[record_ref[0], 1:2], shape)
    for k in range(1, lengths_ref.shape[0]):
        start = start + lengths_ref[k - 1]
        here = flat >= start
        starts = jnp.where(here, start, starts)
        amp = jnp.where(here, recs[record_ref[k], 0:1], amp)
        corr = jnp.where(here, recs[record_ref[k], 1:2], corr)
    return amp, corr, starts.astype(F32), flat - starts


def filter_terms(amp, corr, place, noise):
    a2 = amp * amp
    phi = jnp.exp(-1.0 / corr)
    phi2 = phi * phi
    q = a2 * (1.0 - phi2)
    r = noise * noise
    rp = flat_shift(r, 1)
    first = place == 0
    m11 = jnp.where(first, 0.0, phi2 * rp + q)
    m12 = jnp.where(first, a2, q * rp)
    m21 = jnp.where(first, 0.0, 1.0)
    m22 = jnp.where(first, 1.0, rp)
    d = 1
    while d < LANES:
        n11, n12, n21, n22 = (flat_shift(x, d) for x in (m11, m12, m21, m22))
        p11 = m11 * n11 + m12 * n21
        p12 = m11 * n12 + m12 * n22
        p21 = m21 * n11 + m22 * n21
        p22 = m21 * n12 + m22 * n22
        m11, m12, m21, m22 = p11, p12, p21, p22
        if d in (4, 32):
            scale = 1.0 / (p11 + p12 + p21 + p22)
            m11, m12, m21, m22 = p11 * scale, p12 * scale, p21 * scale, p22 * scale
        d *= 2
    var = m12 / m22
    s = var + r
    inv_s = 1.0 / s
    return lax.rsqrt(s), jnp.log(phi * r * inv_s), phi * var * inv_s


def log_sums(log_g, place):
    total = log_g
    d = 1
    while d < LANES:
        total = total + jnp.where(place >= d, flat_shift(total, d), 0.0)
        d *= 2
    return total - log_g, total


def factor_block(b, other, cols, before, gain, starts):
    sub = before.shape[0]
    a_i = cols[:, b : b + 1]
    s_i = cols[:, sub + b : sub + b + 1]
    t_i = cols[:, 2 * sub + b : 2 * sub + b + 1]
    value = -(s_i * gain[other : other + 1, :]) * jnp.exp(a_i - before[other : other + 1, :])
    live = t_i == starts[other : other + 1, :]
    if other == b:
        i = lax.broadcasted_iota(jnp.int32, (LANES, LANES), 0)
        j = lax.broadcasted_iota(jnp.int32, (LANES, LANES), 1)
        value = jnp.where(live & (j < i), value, jnp.where(i == j, s_i, 0.0))
    else:
        value = jnp.where(live, value, 0.0)
    high = value.astype(BF16)
    low = (value - high.astype(F32)).astype(BF16)
    return high, low


def kernel(
    n,
    amp_ref, corr_ref, lengths_ref, record_ref, noise_ref, rows_ref, cols_ref,
    out_ref,
    held, rows_vm, rows_t, recs, noise_vm, u_ref, lhs,
    local_sem, rec_send, rec_recv, ring_send, ring_recv, sib_send, sib_recv,
):
    me = lax.axis_index("row")
    core = me % 2
    chip = me // 2
    sibling = chip * 2 + 1 - core
    m = n // 2
    pos = jnp.where(chip % 2 == 0, chip // 2, m - 1 - chip // 2)
    obs = rows_ref.shape[0]
    half = obs // 2
    blocks = obs // LANES
    steps = m - 1
    sub = noise_vm.shape[0]

    def device(p, c):
        p = (p + 2 * m) % m
        return jnp.where(p < m // 2, 2 * p, 2 * (m - 1 - p) + 1) * 2 + c

    own_cols = pltpu.make_async_copy(cols_ref, held.at[me], local_sem.at[0])
    own_rows = pltpu.make_async_copy(rows_ref, rows_vm, local_sem.at[1])
    own_cols.start()
    own_rows.start()

    barrier = pltpu.get_barrier_semaphore()

    def greet(o, _):
        pl.semaphore_signal(barrier, inc=1, device_id={"row": (me + o) % n}, device_id_type=MESH)
        return 0

    lax.fori_loop(1, n, greet, 0)
    recs[me, 0:1] = jnp.full((1, LANES), amp_ref[0], F32)
    recs[me, 1:2] = jnp.full((1, LANES), corr_ref[0], F32)
    noise_vm[...] = jnp.ones_like(noise_vm)
    noise_vm[:blocks, :] = noise_ref[...]
    pl.semaphore_wait(barrier, n - 1)

    def record_copy(source, target):
        return pltpu.make_async_remote_copy(
            src_ref=recs.at[source], dst_ref=recs.at[source],
            send_sem=rec_send.at[target], recv_sem=rec_recv.at[source],
            device_id={"row": target}, device_id_type=MESH,
        )

    def send_record(o, _):
        record_copy(me, (me + o) % n).start()
        return 0

    def half_of(direction, h):
        return ((h + direction) % 2) * half

    def sign(direction):
        return 1 - 2 * direction

    def ring_copy(direction, h, q, at, own=False):
        origin = device(at - sign(direction) * (h // 2), core)
        lines = pl.ds(half_of(direction, h) + q * (half // 2), half // 2)
        part = held.at[origin, lines]
        return pltpu.make_async_remote_copy(
            src_ref=cols_ref.at[lines] if own else part, dst_ref=part,
            send_sem=ring_send.at[direction, 2 * h + q], recv_sem=ring_recv.at[direction, 2 * h + q],
            device_id={"row": device(pos + sign(direction), core)}, device_id_type=MESH,
        )

    def sibling_copy(direction, h, c):
        origin = device(pos - sign(direction) * (h // 2 + 1), c)
        part = held.at[origin, pl.ds(half_of(direction, h), half)]
        return pltpu.make_async_remote_copy(
            src_ref=part, dst_ref=part,
            send_sem=sib_send.at[direction, h], recv_sem=sib_recv.at[direction, h],
            device_id={"row": sibling}, device_id_type=MESH,
        )

    def own_copy(c):
        return pltpu.make_async_remote_copy(
            src_ref=cols_ref, dst_ref=held.at[chip * 2 + c],
            send_sem=sib_send.at[0, steps], recv_sem=sib_recv.at[0, steps],
            device_id={"row": sibling}, device_id_type=MESH,
        )

    for direction in range(2):
        ring_copy(direction, 0, 0, pos, True).start()
    lax.fori_loop(1, n, send_record, 0)
    for h, q in ((0, 1), (1, 0), (1, 1)):
        for direction in range(2):
            ring_copy(direction, h, q, pos, True).start()
    own_copy(core).start()

    def pass_on(h, q, more=None):
        more = h + 2 < steps if more is None else more
        for direction in range(2):
            ring_copy(direction, h, q, pos - sign(direction)).wait_recv()
            if more:
                ring_copy(direction, h + 2, q, pos).start()
            if q == 1:
                sibling_copy(direction, h, core).start()

    def take(k):
        for direction in range(2):
            sibling_copy(direction, k, 1 - core).wait_recv()

    def tiles(p):
        block = device(p, 0)
        pair = jnp.concatenate([held[block], held[block + 1]], axis=1)
        both = jnp.dot(lhs[...], pair, preferred_element_type=F32)
        both = both[:LANES] + both[LANES:]
        out_ref[block] = both[:, :LANES]
        out_ref[block + 1] = both[:, LANES:]

    own_rows.wait()
    for b in range(blocks):
        rows_t[:, b * LANES : (b + 1) * LANES] = (
            rows_vm[b * LANES : (b + 1) * LANES, :].astype(F32).T.astype(BF16)
        )
    u_ref[...] = jnp.zeros_like(u_ref)
    pass_on(0, 0)

    def take_record(o, _):
        record_copy((me + o) % n, me).wait_recv()
        return 0

    lax.fori_loop(1, n, take_record, 0)
    amp, corr, starts, place = record_terms(lengths_ref, record_ref, recs, noise_vm.shape)
    scale, log_g, gain = filter_terms(amp, corr, place, noise_vm[...])
    pass_on(0, 1)
    after, before = log_sums(log_g, place)
    cols = jnp.concatenate(
        [after, scale, starts, jnp.zeros((LANES - 3 * sub, LANES), F32)], axis=0
    ).T

    def mix(b):
        near = [b] if b == 0 else [b - 1, b]
        span = slice(near[0] * LANES, (b + 1) * LANES)
        wide = len(near) * LANES
        parts = [factor_block(b, other, cols, before, gain, starts) for other in near]
        both = jnp.concatenate([part[0] for part in parts] + [part[1] for part in parts], axis=1)
        left = rows_t[:, span]
        white = lax.dot_general(
            jnp.concatenate([left, left], axis=1), both, (((1,), (1,)), ((), ())), preferred_element_type=F32
        ).astype(BF16)
        back = jnp.dot(white, both, preferred_element_type=F32)
        u_ref[:, span] += back[:, :wide] + back[:, wide:]

    def tiles_at(d, direction):
        tiles(pos - sign(direction) * d)

    last = m // 2 - 1
    pass_on(1, 0)
    mix(0)
    mix(1)
    pass_on(1, 1)
    mix(2)
    mix(3)
    pass_on(2, 0)
    for b in range(4, blocks):
        mix(b)
    pass_on(2, 1)
    u = u_ref[...]
    high = u.astype(BF16)
    lhs[:LANES, :] = high
    lhs[LANES:, :] = (u - high.astype(F32)).astype(BF16)
    own_copy(1 - core).wait_recv()
    own_cols.wait()
    tiles(pos)
    pass_on(3, 0)
    take(0)
    take(1)
    tiles_at(1, 0)
    pass_on(3, 1)
    tiles_at(1, 1)

    def one(d, more):
        h = 2 * d - 2
        pass_on(h, 0, more)
        take(h - 2)
        take(h - 1)
        tiles_at(d - 1, 0)
        pass_on(h, 1, more)
        tiles_at(d - 1, 1)
        pass_on(h + 1, 0, more)
        pass_on(h + 1, 1, more)

    if last > 3:
        def body(d, _):
            one(d, True)
            return 0

        lax.fori_loop(3, last, body, 0)
    one(last, None)
    pass_on(steps - 1, 0)
    take(steps - 3)
    take(steps - 2)
    tiles_at(last, 0)
    pass_on(steps - 1, 1)
    tiles_at(last, 1)
    take(steps - 1)
    tiles(pos + m // 2)

    def left(h, own=False):
        for direction in range(2):
            for q in range(2):
                ring_copy(direction, h, q, pos, own).wait_send()
            sibling_copy(direction, h, core).wait_send()

    def rest_left(h, _):
        left(h)
        return 0

    left(0, True)
    left(1, True)
    lax.fori_loop(2, steps, rest_left, 0)
    own_copy(core).wait_send()

    def record_left(o, _):
        record_copy(me, (me + o) % n).wait_send()
        return 0

    lax.fori_loop(1, n, record_left, 0)


def gather_multiply(n, amp, corr, lengths, record, noise, rows, cols):
    obs, width = cols.shape
    sub = -(-noise.shape[0] // 8) * 8
    steps = n // 2 - 1
    smem = pl.BlockSpec(memory_space=pltpu.SMEM)
    vmem = pl.BlockSpec(memory_space=pltpu.VMEM)
    hbm = pl.BlockSpec(memory_space=pltpu.HBM)
    dma = pltpu.SemaphoreType.DMA
    return pl.pallas_call(
        functools.partial(kernel, n),
        out_shape=pltpu.VMEM((n, rows.shape[1], width), F32),
        in_specs=[smem, smem, smem, smem, vmem, hbm, hbm],
        out_specs=vmem,
        scratch_shapes=[
            pltpu.VMEM((n, obs, width), BF16),
            pltpu.VMEM((obs, LANES), BF16),
            pltpu.VMEM((LANES, obs), BF16),
            pltpu.VMEM((n, 8, LANES), F32),
            pltpu.VMEM((sub, LANES), F32),
            pltpu.VMEM((LANES, obs), F32),
            pltpu.VMEM((2 * LANES, obs), BF16),
            dma((2,)),
            dma((n,)),
            dma((n,)),
            dma((2, 2 * steps)),
            dma((2, 2 * steps)),
            dma((2, steps + 1)),
            dma((2, steps + 1)),
        ],
        compiler_params=pltpu.CompilerParams(
            collective_id=0, has_side_effects=True, vmem_limit_bytes=54 * 1024 * 1024
        ),
    )(amp, corr, lengths, record, noise, rows, cols)


def place_kernel(map_ref, tiles_ref, out_ref, sems):
    count, _, width = tiles_ref.shape

    def put(j):
        return pltpu.make_async_copy(
            tiles_ref.at[map_ref[j]], out_ref.at[:, pl.ds(j * width, width)], sems.at[j]
        )

    for j in range(count):
        put(j).start()
    for j in range(count):
        put(j).wait()


def place_blocks(block_map, tiles):
    count, height, width = tiles.shape
    return pl.pallas_call(
        place_kernel,
        out_shape=jax.ShapeDtypeStruct((height, count * width), F32),
        in_specs=[pl.BlockSpec(memory_space=pltpu.SMEM), pl.BlockSpec(memory_space=pltpu.VMEM)],
        out_specs=pl.BlockSpec(memory_space=pl.ANY),
        scratch_shapes=[pltpu.SemaphoreType.DMA((count,))],
        compiler_params=pltpu.CompilerParams(vmem_limit_bytes=16 * 1024 * 1024),
    )(block_map, tiles)


def per_device(
    design_rows,
    design_cols,
    noise_std,
    record_noise_amplitude,
    record_correlation_length,
    arc_lengths,
    arc_record_index,
    block_map,
):
    n = lax.axis_size("row")
    noise = noise_std.reshape(-1, LANES)
    tiles = gather_multiply(
        n,
        record_noise_amplitude,
        record_correlation_length,
        arc_lengths,
        arc_record_index,
        noise,
        design_rows,
        design_cols,
    )
    return place_blocks(block_map, tiles)


def solution(mesh):
    return jax.shard_map(
        per_device,
        mesh=mesh,
        in_specs=(
            P("groups", "row"),
            P("groups", "row"),
            P("groups"),
            P(("groups", "row")),
            P(("groups", "row")),
            P("groups"),
            P("groups"),
            P("groups"),
        ),
        out_specs=P(("groups", "row"), None),
        check_vma=False,
    )
```

```python
import functools

import jax
import jax.numpy as jnp
from jax import lax
from jax.experimental import pallas as pl
from jax.experimental.pallas import tpu as pltpu
from jax.sharding import PartitionSpec as P

LANES = 128
MESH = pl.DeviceIdType.MESH
F32 = jnp.float32
BF16 = jnp.bfloat16


def flat_shift(x, d):
    rolled = pltpu.roll(x, d, 1)
    above = pltpu.roll(rolled, 1, 0)
    lane = lax.broadcasted_iota(jnp.int32, x.shape, 1)
    return jnp.where(lane < d, above, rolled)


def record_terms(lengths_ref, record_ref, recs, shape):
    flat = lax.broadcasted_iota(jnp.int32, shape, 0) * LANES + lax.broadcasted_iota(jnp.int32, shape, 1)
    start = jnp.int32(0)
    starts = jnp.zeros(shape, jnp.int32)
    amp = jnp.broadcast_to(recs[record_ref[0], 0:1], shape)
    corr = jnp.broadcast_to(recs[record_ref[0], 1:2], shape)
    for k in range(1, lengths_ref.shape[0]):
        start = start + lengths_ref[k - 1]
        here = flat >= start
        starts = jnp.where(here, start, starts)
        amp = jnp.where(here, recs[record_ref[k], 0:1], amp)
        corr = jnp.where(here, recs[record_ref[k], 1:2], corr)
    return amp, corr, starts.astype(F32), flat - starts


def filter_terms(amp, corr, place, noise):
    a2 = amp * amp
    phi = jnp.exp(-1.0 / corr)
    phi2 = phi * phi
    q = a2 * (1.0 - phi2)
    r = noise * noise
    rp = flat_shift(r, 1)
    first = place == 0
    m11 = jnp.where(first, 0.0, phi2 * rp + q)
    m12 = jnp.where(first, a2, q * rp)
    m21 = jnp.where(first, 0.0, 1.0)
    m22 = jnp.where(first, 1.0, rp)
    d = 1
    while d < LANES:
        n11, n12, n21, n22 = (flat_shift(x, d) for x in (m11, m12, m21, m22))
        p11 = m11 * n11 + m12 * n21
        p12 = m11 * n12 + m12 * n22
        p21 = m21 * n11 + m22 * n21
        p22 = m21 * n12 + m22 * n22
        m11, m12, m21, m22 = p11, p12, p21, p22
        if d in (4, 32):
            scale = 1.0 / (p11 + p12 + p21 + p22)
            m11, m12, m21, m22 = p11 * scale, p12 * scale, p21 * scale, p22 * scale
        d *= 2
    var = m12 / m22
    s = var + r
    inv_s = 1.0 / s
    return lax.rsqrt(s), jnp.log(phi * r * inv_s), phi * var * inv_s


def log_sums(log_g, place):
    total = log_g
    d = 1
    while d < LANES:
        total = total + jnp.where(place >= d, flat_shift(total, d), 0.0)
        d *= 2
    return total - log_g, total


def factor_block(b, other, cols, before, gain, starts):
    sub = before.shape[0]
    a_i = cols[:, b : b + 1]
    s_i = cols[:, sub + b : sub + b + 1]
    t_i = cols[:, 2 * sub + b : 2 * sub + b + 1]
    value = -(s_i * gain[other : other + 1, :]) * jnp.exp(a_i - before[other : other + 1, :])
    live = t_i == starts[other : other + 1, :]
    if other == b:
        i = lax.broadcasted_iota(jnp.int32, (LANES, LANES), 0)
        j = lax.broadcasted_iota(jnp.int32, (LANES, LANES), 1)
        value = jnp.where(live & (j < i), value, jnp.where(i == j, s_i, 0.0))
    else:
        value = jnp.where(live, value, 0.0)
    high = value.astype(BF16)
    low = (value - high.astype(F32)).astype(BF16)
    return high, low


def kernel(
    n,
    amp_ref, corr_ref, lengths_ref, record_ref, map_ref, noise_ref, rows_ref, cols_ref,
    out_ref,
    held, product, rows_vm, rows_t, recs, noise_vm, u_ref, lhs,
    local_sem, rec_send, rec_recv, ring_send, ring_recv, sib_send, sib_recv,
):
    me = lax.axis_index("row")
    core = me % 2
    chip = me // 2
    sibling = chip * 2 + 1 - core
    m = n // 2
    pos = jnp.where(chip % 2 == 0, chip // 2, m - 1 - chip // 2)
    obs = rows_ref.shape[0]
    half = obs // 2
    blocks = obs // LANES
    steps = m - 1
    sub = noise_vm.shape[0]

    def device(p, c):
        p = (p + 2 * m) % m
        return jnp.where(p < m // 2, 2 * p, 2 * (m - 1 - p) + 1) * 2 + c

    own_cols = pltpu.make_async_copy(cols_ref, held.at[me], local_sem.at[0])
    own_rows = pltpu.make_async_copy(rows_ref, rows_vm, local_sem.at[1])
    own_cols.start()
    own_rows.start()

    barrier = pltpu.get_barrier_semaphore()

    def greet(o, _):
        pl.semaphore_signal(barrier, inc=1, device_id={"row": (me + o) % n}, device_id_type=MESH)
        return 0

    lax.fori_loop(1, n, greet, 0)
    recs[me, 0:1] = jnp.full((1, LANES), amp_ref[0], F32)
    recs[me, 1:2] = jnp.full((1, LANES), corr_ref[0], F32)
    noise_vm[...] = jnp.ones_like(noise_vm)
    noise_vm[:blocks, :] = noise_ref[...]
    pl.semaphore_wait(barrier, n - 1)

    def record_copy(source, target):
        return pltpu.make_async_remote_copy(
            src_ref=recs.at[source], dst_ref=recs.at[source],
            send_sem=rec_send.at[target], recv_sem=rec_recv.at[source],
            device_id={"row": target}, device_id_type=MESH,
        )

    def send_record(o, _):
        record_copy(me, (me + o) % n).start()
        return 0

    def half_of(direction, h):
        return ((h + direction) % 2) * half

    def sign(direction):
        return 1 - 2 * direction

    def ring_copy(direction, h, q, at, own=False):
        origin = device(at - sign(direction) * (h // 2), core)
        lines = pl.ds(half_of(direction, h) + q * (half // 2), half // 2)
        part = held.at[origin, lines]
        return pltpu.make_async_remote_copy(
            src_ref=cols_ref.at[lines] if own else part, dst_ref=part,
            send_sem=ring_send.at[direction, 2 * h + q], recv_sem=ring_recv.at[direction, 2 * h + q],
            device_id={"row": device(pos + sign(direction), core)}, device_id_type=MESH,
        )

    def sibling_copy(direction, h, c):
        origin = device(pos - sign(direction) * (h // 2 + 1), c)
        part = held.at[origin, pl.ds(half_of(direction, h), half)]
        return pltpu.make_async_remote_copy(
            src_ref=part, dst_ref=part,
            send_sem=sib_send.at[direction, h], recv_sem=sib_recv.at[direction, h],
            device_id={"row": sibling}, device_id_type=MESH,
        )

    def own_copy(c):
        return pltpu.make_async_remote_copy(
            src_ref=cols_ref, dst_ref=held.at[chip * 2 + c],
            send_sem=sib_send.at[0, steps], recv_sem=sib_recv.at[0, steps],
            device_id={"row": sibling}, device_id_type=MESH,
        )

    lax.fori_loop(1, n, send_record, 0)
    for h, q in ((0, 0), (0, 1), (1, 0), (1, 1)):
        for direction in range(2):
            ring_copy(direction, h, q, pos, True).start()
    own_copy(core).start()

    def pass_on(h, q, more=None):
        more = h + 2 < steps if more is None else more
        for direction in range(2):
            ring_copy(direction, h, q, pos - sign(direction)).wait_recv()
            if more:
                ring_copy(direction, h + 2, q, pos).start()
            if q == 1:
                sibling_copy(direction, h, core).start()

    def take(k):
        for direction in range(2):
            sibling_copy(direction, k, 1 - core).wait_recv()

    def tiles(p):
        block = device(p, 0)
        pair = jnp.concatenate([held[block], held[block + 1]], axis=1)
        both = jnp.dot(lhs[...], pair, preferred_element_type=F32)
        both = both[:LANES] + both[LANES:]
        product[block] = both[:, :LANES]
        product[block + 1] = both[:, LANES:]

    own_rows.wait()
    for b in range(blocks):
        rows_t[:, b * LANES : (b + 1) * LANES] = (
            rows_vm[b * LANES : (b + 1) * LANES, :].astype(F32).T.astype(BF16)
        )
    u_ref[...] = jnp.zeros_like(u_ref)
    pass_on(0, 0)

    def take_record(o, _):
        record_copy((me + o) % n, me).wait_recv()
        return 0

    lax.fori_loop(1, n, take_record, 0)
    amp, corr, starts, place = record_terms(lengths_ref, record_ref, recs, noise_vm.shape)
    scale, log_g, gain = filter_terms(amp, corr, place, noise_vm[...])
    pass_on(0, 1)
    after, before = log_sums(log_g, place)
    cols = jnp.concatenate(
        [after, scale, starts, jnp.zeros((LANES - 3 * sub, LANES), F32)], axis=0
    ).T

    def mix(b):
        near = [b] if b == 0 else [b - 1, b]
        span = slice(near[0] * LANES, (b + 1) * LANES)
        wide = len(near) * LANES
        parts = [factor_block(b, other, cols, before, gain, starts) for other in near]
        both = jnp.concatenate([part[0] for part in parts] + [part[1] for part in parts], axis=1)
        left = rows_t[:, span]
        white = lax.dot_general(
            jnp.concatenate([left, left], axis=1), both, (((1,), (1,)), ((), ())), preferred_element_type=F32
        ).astype(BF16)
        back = jnp.dot(white, both, preferred_element_type=F32)
        u_ref[:, span] += back[:, :wide] + back[:, wide:]

    def tiles_at(d, direction):
        tiles(pos - sign(direction) * d)

    last = m // 2 - 1
    pass_on(1, 0)
    mix(0)
    mix(1)
    pass_on(1, 1)
    mix(2)
    mix(3)
    pass_on(2, 0)
    for b in range(4, blocks):
        mix(b)
    pass_on(2, 1)
    u = u_ref[...]
    high = u.astype(BF16)
    lhs[:LANES, :] = high
    lhs[LANES:, :] = (u - high.astype(F32)).astype(BF16)
    own_copy(1 - core).wait_recv()
    own_cols.wait()
    tiles(pos)
    pass_on(3, 0)
    take(0)
    take(1)
    tiles_at(1, 0)
    pass_on(3, 1)
    tiles_at(1, 1)

    def one(d, more):
        h = 2 * d - 2
        pass_on(h, 0, more)
        take(h - 2)
        take(h - 1)
        tiles_at(d - 1, 0)
        pass_on(h, 1, more)
        tiles_at(d - 1, 1)
        pass_on(h + 1, 0, more)
        pass_on(h + 1, 1, more)

    if last > 3:
        def body(d, _):
            one(d, True)
            return 0

        lax.fori_loop(3, last, body, 0)
    one(last, None)
    pass_on(steps - 1, 0)
    take(steps - 3)
    take(steps - 2)
    tiles_at(last, 0)
    pass_on(steps - 1, 1)
    tiles_at(last, 1)
    take(steps - 1)
    tiles(pos + m // 2)

    for j in range(n):
        out_ref[:, j * LANES : (j + 1) * LANES] = product[map_ref[j]]

    def left(h, own=False):
        for direction in range(2):
            for q in range(2):
                ring_copy(direction, h, q, pos, own).wait_send()
            sibling_copy(direction, h, core).wait_send()

    def rest_left(h, _):
        left(h)
        return 0

    left(0, True)
    left(1, True)
    lax.fori_loop(2, steps, rest_left, 0)
    own_copy(core).wait_send()

    def record_left(o, _):
        record_copy(me, (me + o) % n).wait_send()
        return 0

    lax.fori_loop(1, n, record_left, 0)


def gather_multiply(n, amp, corr, lengths, record, block_map, noise, rows, cols):
    obs, width = cols.shape
    sub = -(-noise.shape[0] // 8) * 8
    steps = n // 2 - 1
    smem = pl.BlockSpec(memory_space=pltpu.SMEM)
    vmem = pl.BlockSpec(memory_space=pltpu.VMEM)
    hbm = pl.BlockSpec(memory_space=pltpu.HBM)
    dma = pltpu.SemaphoreType.DMA
    return pl.pallas_call(
        functools.partial(kernel, n),
        out_shape=pltpu.VMEM((rows.shape[1], n * width), F32),
        in_specs=[smem, smem, smem, smem, smem, vmem, hbm, hbm],
        out_specs=vmem,
        scratch_shapes=[
            pltpu.VMEM((n, obs, width), BF16),
            pltpu.VMEM((n, LANES, width), F32),
            pltpu.VMEM((obs, LANES), BF16),
            pltpu.VMEM((LANES, obs), BF16),
            pltpu.VMEM((n, 8, LANES), F32),
            pltpu.VMEM((sub, LANES), F32),
            pltpu.VMEM((LANES, obs), F32),
            pltpu.VMEM((2 * LANES, obs), BF16),
            dma((2,)),
            dma((n,)),
            dma((n,)),
            dma((2, 2 * steps)),
            dma((2, 2 * steps)),
            dma((2, steps + 1)),
            dma((2, steps + 1)),
        ],
        compiler_params=pltpu.CompilerParams(
            collective_id=0, has_side_effects=True, vmem_limit_bytes=54 * 1024 * 1024
        ),
    )(amp, corr, lengths, record, block_map, noise, rows, cols)


def per_device(
    design_rows,
    design_cols,
    noise_std,
    record_noise_amplitude,
    record_correlation_length,
    arc_lengths,
    arc_record_index,
    block_map,
):
    n = lax.axis_size("row")
    noise = noise_std.reshape(-1, LANES)
    return gather_multiply(
        n,
        record_noise_amplitude,
        record_correlation_length,
        arc_lengths,
        arc_record_index,
        block_map,
        noise,
        design_rows,
        design_cols,
    )


def solution(mesh):
    return jax.shard_map(
        per_device,
        mesh=mesh,
        in_specs=(
            P("groups", "row"),
            P("groups", "row"),
            P("groups"),
            P(("groups", "row")),
            P(("groups", "row")),
            P("groups"),
            P("groups"),
            P("groups"),
        ),
        out_specs=P(("groups", "row"), None),
        check_vma=False,
    )
```

```python
import functools

import jax
import jax.numpy as jnp
from jax import lax
from jax.experimental import pallas as pl
from jax.experimental.pallas import tpu as pltpu
from jax.sharding import PartitionSpec as P

LANES = 128
MESH = pl.DeviceIdType.MESH
F32 = jnp.float32
BF16 = jnp.bfloat16


def flat_shift(x, d):
    rolled = pltpu.roll(x, d, 1)
    above = pltpu.roll(rolled, 1, 0)
    lane = lax.broadcasted_iota(jnp.int32, x.shape, 1)
    return jnp.where(lane < d, above, rolled)


def record_terms(lengths_ref, record_ref, recs, shape):
    flat = lax.broadcasted_iota(jnp.int32, shape, 0) * LANES + lax.broadcasted_iota(jnp.int32, shape, 1)
    start = jnp.int32(0)
    starts = jnp.zeros(shape, jnp.int32)
    amp = jnp.broadcast_to(recs[record_ref[0], 0:1], shape)
    corr = jnp.broadcast_to(recs[record_ref[0], 1:2], shape)
    for k in range(1, lengths_ref.shape[0]):
        start = start + lengths_ref[k - 1]
        here = flat >= start
        starts = jnp.where(here, start, starts)
        amp = jnp.where(here, recs[record_ref[k], 0:1], amp)
        corr = jnp.where(here, recs[record_ref[k], 1:2], corr)
    return amp, corr, starts.astype(F32), flat - starts


def filter_terms(amp, corr, place, noise):
    a2 = amp * amp
    phi = jnp.exp(-1.0 / corr)
    phi2 = phi * phi
    q = a2 * (1.0 - phi2)
    r = noise * noise
    rp = flat_shift(r, 1)
    first = place == 0
    m11 = jnp.where(first, 0.0, phi2 * rp + q)
    m12 = jnp.where(first, a2, q * rp)
    m21 = jnp.where(first, 0.0, 1.0)
    m22 = jnp.where(first, 1.0, rp)
    d = 1
    while d < LANES:
        n11, n12, n21, n22 = (flat_shift(x, d) for x in (m11, m12, m21, m22))
        p11 = m11 * n11 + m12 * n21
        p12 = m11 * n12 + m12 * n22
        p21 = m21 * n11 + m22 * n21
        p22 = m21 * n12 + m22 * n22
        m11, m12, m21, m22 = p11, p12, p21, p22
        if d in (4, 32):
            scale = 1.0 / (p11 + p12 + p21 + p22)
            m11, m12, m21, m22 = p11 * scale, p12 * scale, p21 * scale, p22 * scale
        d *= 2
    var = m12 / m22
    s = var + r
    inv_s = 1.0 / s
    return lax.rsqrt(s), jnp.log(phi * r * inv_s), phi * var * inv_s


def log_sums(log_g, place):
    total = log_g
    d = 1
    while d < LANES:
        total = total + jnp.where(place >= d, flat_shift(total, d), 0.0)
        d *= 2
    return total - log_g, total


def factor_block(b, other, cols, before, gain, starts):
    sub = before.shape[0]
    a_i = cols[:, b : b + 1]
    s_i = cols[:, sub + b : sub + b + 1]
    t_i = cols[:, 2 * sub + b : 2 * sub + b + 1]
    value = -(s_i * gain[other : other + 1, :]) * jnp.exp(a_i - before[other : other + 1, :])
    live = t_i == starts[other : other + 1, :]
    if other == b:
        i = lax.broadcasted_iota(jnp.int32, (LANES, LANES), 0)
        j = lax.broadcasted_iota(jnp.int32, (LANES, LANES), 1)
        value = jnp.where(live & (j < i), value, jnp.where(i == j, s_i, 0.0))
    else:
        value = jnp.where(live, value, 0.0)
    high = value.astype(BF16)
    low = (value - high.astype(F32)).astype(BF16)
    return high, low


def kernel(
    n,
    amp_ref, corr_ref, lengths_ref, record_ref, map_ref, noise_ref, rows_ref, cols_ref,
    out_ref,
    held, product, rows_vm, rows_t, recs, noise_vm, u_ref, lhs,
    local_sem, rec_send, rec_recv, ring_send, ring_recv, sib_send, sib_recv,
):
    me = lax.axis_index("row")
    core = me % 2
    chip = me // 2
    sibling = chip * 2 + 1 - core
    m = n // 2
    pos = jnp.where(chip % 2 == 0, chip // 2, m - 1 - chip // 2)
    obs = rows_ref.shape[0]
    half = obs // 2
    blocks = obs // LANES
    steps = m - 1
    sub = noise_vm.shape[0]

    def device(p, c):
        p = (p + 2 * m) % m
        return jnp.where(p < m // 2, 2 * p, 2 * (m - 1 - p) + 1) * 2 + c

    after_me, before_me = device(pos + 1, core), device(pos - 1, core)
    own_cols = pltpu.make_async_copy(cols_ref, held.at[me], local_sem.at[0])
    own_rows = pltpu.make_async_copy(rows_ref, rows_vm, local_sem.at[1])
    own_cols.start()
    own_rows.start()

    barrier = pltpu.get_barrier_semaphore()

    def greet(o, _):
        pl.semaphore_signal(barrier, inc=1, device_id={"row": (me + o) % n}, device_id_type=MESH)
        return 0

    lax.fori_loop(1, n, greet, 0)
    recs[me, 0:1] = jnp.full((1, LANES), amp_ref[0], F32)
    recs[me, 1:2] = jnp.full((1, LANES), corr_ref[0], F32)
    noise_vm[...] = jnp.ones_like(noise_vm)
    noise_vm[:blocks, :] = noise_ref[...]
    pl.semaphore_wait(barrier, n - 1)

    def record_copy(source, target):
        return pltpu.make_async_remote_copy(
            src_ref=recs.at[source], dst_ref=recs.at[source],
            send_sem=rec_send, recv_sem=rec_recv,
            device_id={"row": target}, device_id_type=MESH,
        )

    def records(count):
        part = recs.at[pl.ds(0, count)]
        return pltpu.make_async_remote_copy(
            src_ref=part, dst_ref=part, send_sem=rec_send, recv_sem=rec_recv,
            device_id={"row": sibling}, device_id_type=MESH,
        )

    def all_sent(count, sem):
        part = held.at[pl.ds(0, count)]
        pltpu.make_async_remote_copy(
            src_ref=part, dst_ref=part, send_sem=sem, recv_sem=sib_recv.at[0, steps],
            device_id={"row": sibling}, device_id_type=MESH,
        ).wait_send()

    def send_record(o, _):
        record_copy(me, (me + o) % n).start()
        return 0

    def half_of(direction, h):
        return ((h + direction) % 2) * half

    def sign(direction):
        return 1 - 2 * direction

    def ring_copy(direction, h, q, at, own=False):
        origin = device(at - sign(direction) * (h // 2), core)
        lines = pl.ds(half_of(direction, h) + q * (half // 2), half // 2)
        part = held.at[origin, lines]
        return pltpu.make_async_remote_copy(
            src_ref=cols_ref.at[lines] if own else part, dst_ref=part,
            send_sem=ring_send, recv_sem=ring_recv.at[direction, 2 * h + q],
            device_id={"row": after_me if direction == 0 else before_me}, device_id_type=MESH,
        )

    def sibling_copy(direction, h, c):
        origin = device(pos - sign(direction) * (h // 2 + 1), c)
        part = held.at[origin, pl.ds(half_of(direction, h), half)]
        return pltpu.make_async_remote_copy(
            src_ref=part, dst_ref=part,
            send_sem=sib_send, recv_sem=sib_recv.at[direction, h],
            device_id={"row": sibling}, device_id_type=MESH,
        )

    def own_copy(c):
        return pltpu.make_async_remote_copy(
            src_ref=cols_ref, dst_ref=held.at[chip * 2 + c],
            send_sem=sib_send, recv_sem=sib_recv.at[0, steps],
            device_id={"row": sibling}, device_id_type=MESH,
        )

    lax.fori_loop(1, n, send_record, 0)
    for h, q in ((0, 0), (0, 1), (1, 0), (1, 1)):
        for direction in range(2):
            ring_copy(direction, h, q, pos, True).start()
    own_copy(core).start()

    def pass_on(h, q, more=None):
        more = h + 2 < steps if more is None else more
        for direction in range(2):
            ring_copy(direction, h, q, pos - sign(direction)).wait_recv()
            if more:
                ring_copy(direction, h + 2, q, pos).start()
            if q == 1:
                sibling_copy(direction, h, core).start()

    def take(k):
        for direction in range(2):
            sibling_copy(direction, k, 1 - core).wait_recv()

    def tiles(p):
        block = device(p, 0)
        pair = jnp.concatenate([held[block], held[block + 1]], axis=1)
        both = jnp.dot(lhs[...], pair, preferred_element_type=F32)
        both = both[:LANES] + both[LANES:]
        product[block] = both[:, :LANES]
        product[block + 1] = both[:, LANES:]

    own_rows.wait()
    for b in range(blocks):
        rows_t[:, b * LANES : (b + 1) * LANES] = (
            rows_vm[b * LANES : (b + 1) * LANES, :].astype(F32).T.astype(BF16)
        )
    u_ref[...] = jnp.zeros_like(u_ref)
    pass_on(0, 0)

    records(n - 1).wait_recv()
    amp, corr, starts, place = record_terms(lengths_ref, record_ref, recs, noise_vm.shape)
    scale, log_g, gain = filter_terms(amp, corr, place, noise_vm[...])
    pass_on(0, 1)
    after, before = log_sums(log_g, place)
    cols = jnp.concatenate(
        [after, scale, starts, jnp.zeros((LANES - 3 * sub, LANES), F32)], axis=0
    ).T

    def mix(b):
        near = [b] if b == 0 else [b - 1, b]
        span = slice(near[0] * LANES, (b + 1) * LANES)
        wide = len(near) * LANES
        parts = [factor_block(b, other, cols, before, gain, starts) for other in near]
        both = jnp.concatenate([part[0] for part in parts] + [part[1] for part in parts], axis=1)
        left = rows_t[:, span]
        white = lax.dot_general(
            jnp.concatenate([left, left], axis=1), both, (((1,), (1,)), ((), ())), preferred_element_type=F32
        ).astype(BF16)
        back = jnp.dot(white, both, preferred_element_type=F32)
        u_ref[:, span] += back[:, :wide] + back[:, wide:]

    def tiles_at(d, direction):
        tiles(pos - sign(direction) * d)

    last = m // 2 - 1
    pass_on(1, 0)
    mix(0)
    mix(1)
    pass_on(1, 1)
    mix(2)
    mix(3)
    pass_on(2, 0)
    for b in range(4, blocks):
        mix(b)
    pass_on(2, 1)
    u = u_ref[...]
    high = u.astype(BF16)
    lhs[:LANES, :] = high
    lhs[LANES:, :] = (u - high.astype(F32)).astype(BF16)
    own_copy(1 - core).wait_recv()
    own_cols.wait()
    tiles(pos)
    pass_on(3, 0)
    take(0)
    take(1)
    tiles_at(1, 0)
    pass_on(3, 1)
    tiles_at(1, 1)

    def one(d, more):
        h = 2 * d - 2
        pass_on(h, 0, more)
        take(h - 2)
        take(h - 1)
        tiles_at(d - 1, 0)
        pass_on(h, 1, more)
        tiles_at(d - 1, 1)
        pass_on(h + 1, 0, more)
        pass_on(h + 1, 1, more)

    if last > 3:
        def body(d, _):
            one(d, True)
            return 0

        lax.fori_loop(3, last, body, 0)
    one(last, None)
    pass_on(steps - 1, 0)
    take(steps - 3)
    take(steps - 2)
    tiles_at(last, 0)
    pass_on(steps - 1, 1)
    tiles_at(last, 1)
    take(steps - 1)
    tiles(pos + m // 2)

    for j in range(n):
        out_ref[:, j * LANES : (j + 1) * LANES] = product[map_ref[j]]

    all_sent(m - 1, ring_send)
    all_sent(m, sib_send)
    records(n - 1).wait_send()


def gather_multiply(n, amp, corr, lengths, record, block_map, noise, rows, cols):
    obs, width = cols.shape
    sub = -(-noise.shape[0] // 8) * 8
    steps = n // 2 - 1
    smem = pl.BlockSpec(memory_space=pltpu.SMEM)
    vmem = pl.BlockSpec(memory_space=pltpu.VMEM)
    hbm = pl.BlockSpec(memory_space=pltpu.HBM)
    dma = pltpu.SemaphoreType.DMA
    return pl.pallas_call(
        functools.partial(kernel, n),
        out_shape=pltpu.VMEM((rows.shape[1], n * width), F32),
        in_specs=[smem, smem, smem, smem, smem, vmem, hbm, hbm],
        out_specs=vmem,
        scratch_shapes=[
            pltpu.VMEM((n, obs, width), BF16),
            pltpu.VMEM((n, LANES, width), F32),
            pltpu.VMEM((obs, LANES), BF16),
            pltpu.VMEM((LANES, obs), BF16),
            pltpu.VMEM((n, 8, LANES), F32),
            pltpu.VMEM((sub, LANES), F32),
            pltpu.VMEM((LANES, obs), F32),
            pltpu.VMEM((2 * LANES, obs), BF16),
            dma((2,)),
            dma,
            dma,
            dma,
            dma((2, 2 * steps)),
            dma,
            dma((2, steps + 1)),
        ],
        compiler_params=pltpu.CompilerParams(
            collective_id=0, has_side_effects=True, vmem_limit_bytes=54 * 1024 * 1024
        ),
    )(amp, corr, lengths, record, block_map, noise, rows, cols)


def per_device(
    design_rows,
    design_cols,
    noise_std,
    record_noise_amplitude,
    record_correlation_length,
    arc_lengths,
    arc_record_index,
    block_map,
):
    n = lax.axis_size("row")
    noise = noise_std.reshape(-1, LANES)
    return gather_multiply(
        n,
        record_noise_amplitude,
        record_correlation_length,
        arc_lengths,
        arc_record_index,
        block_map,
        noise,
        design_rows,
        design_cols,
    )


def solution(mesh):
    return jax.shard_map(
        per_device,
        mesh=mesh,
        in_specs=(
            P("groups", "row"),
            P("groups", "row"),
            P("groups"),
            P(("groups", "row")),
            P(("groups", "row")),
            P("groups"),
            P("groups"),
            P("groups"),
        ),
        out_specs=P(("groups", "row"), None),
        check_vma=False,
    )
```

```python
import functools

import jax
import jax.numpy as jnp
from jax import lax
from jax.experimental import pallas as pl
from jax.experimental.pallas import tpu as pltpu
from jax.sharding import PartitionSpec as P

LANES = 128
MESH = pl.DeviceIdType.MESH
F32 = jnp.float32
BF16 = jnp.bfloat16


def flat_shift(x, d):
    rolled = pltpu.roll(x, d, 1)
    above = pltpu.roll(rolled, 1, 0)
    lane = lax.broadcasted_iota(jnp.int32, x.shape, 1)
    return jnp.where(lane < d, above, rolled)


def record_terms(lengths_ref, record_ref, recs, shape):
    flat = lax.broadcasted_iota(jnp.int32, shape, 0) * LANES + lax.broadcasted_iota(jnp.int32, shape, 1)
    start = jnp.int32(0)
    starts = jnp.zeros(shape, jnp.int32)
    amp = jnp.broadcast_to(recs[record_ref[0], 0:1], shape)
    corr = jnp.broadcast_to(recs[record_ref[0], 1:2], shape)
    for k in range(1, lengths_ref.shape[0]):
        start = start + lengths_ref[k - 1]
        here = flat >= start
        starts = jnp.where(here, start, starts)
        amp = jnp.where(here, recs[record_ref[k], 0:1], amp)
        corr = jnp.where(here, recs[record_ref[k], 1:2], corr)
    return amp, corr, starts.astype(F32), flat - starts


def filter_terms(amp, corr, place, noise):
    a2 = amp * amp
    phi = jnp.exp(-1.0 / corr)
    phi2 = phi * phi
    q = a2 * (1.0 - phi2)
    r = noise * noise
    rp = flat_shift(r, 1)
    first = place == 0
    m11 = jnp.where(first, 0.0, phi2 * rp + q)
    m12 = jnp.where(first, a2, q * rp)
    m21 = jnp.where(first, 0.0, 1.0)
    m22 = jnp.where(first, 1.0, rp)
    d = 1
    while d < LANES:
        n11, n12, n21, n22 = (flat_shift(x, d) for x in (m11, m12, m21, m22))
        p11 = m11 * n11 + m12 * n21
        p12 = m11 * n12 + m12 * n22
        p21 = m21 * n11 + m22 * n21
        p22 = m21 * n12 + m22 * n22
        m11, m12, m21, m22 = p11, p12, p21, p22
        if d in (4, 32):
            scale = 1.0 / (p11 + p12 + p21 + p22)
            m11, m12, m21, m22 = p11 * scale, p12 * scale, p21 * scale, p22 * scale
        d *= 2
    var = m12 / m22
    s = var + r
    inv_s = 1.0 / s
    return lax.rsqrt(s), jnp.log(phi * r * inv_s), phi * var * inv_s


def log_sums(log_g, place):
    total = log_g
    d = 1
    while d < LANES:
        total = total + jnp.where(place >= d, flat_shift(total, d), 0.0)
        d *= 2
    return total - log_g, total


def factor_block(b, other, cols, before, gain, starts):
    sub = before.shape[0]
    a_i = cols[:, b : b + 1]
    s_i = cols[:, sub + b : sub + b + 1]
    t_i = cols[:, 2 * sub + b : 2 * sub + b + 1]
    value = -(s_i * gain[other : other + 1, :]) * jnp.exp(a_i - before[other : other + 1, :])
    live = t_i == starts[other : other + 1, :]
    if other == b:
        i = lax.broadcasted_iota(jnp.int32, (LANES, LANES), 0)
        j = lax.broadcasted_iota(jnp.int32, (LANES, LANES), 1)
        value = jnp.where(live & (j < i), value, jnp.where(i == j, s_i, 0.0))
    else:
        value = jnp.where(live, value, 0.0)
    high = value.astype(BF16)
    low = (value - high.astype(F32)).astype(BF16)
    return high, low


def kernel(
    n,
    amp_ref, corr_ref, lengths_ref, record_ref, map_ref, noise_ref, rows_ref, cols_ref,
    out_ref,
    held, product, rows_vm, rows_t, recs, noise_vm, u_ref, lhs,
    local_sem, rec_send, rec_recv, rec_sib, ring_send, ring_recv, sib_send, sib_recv,
):
    me = lax.axis_index("row")
    core = me % 2
    chip = me // 2
    sibling = chip * 2 + 1 - core
    m = n // 2
    pos = jnp.where(chip % 2 == 0, chip // 2, m - 1 - chip // 2)
    obs = rows_ref.shape[0]
    half = obs // 2
    blocks = obs // LANES
    steps = m - 1
    sub = noise_vm.shape[0]

    def device(p, c):
        p = (p + 2 * m) % m
        return jnp.where(p < m // 2, 2 * p, 2 * (m - 1 - p) + 1) * 2 + c

    after_me, before_me = device(pos + 1, core), device(pos - 1, core)
    own_cols = pltpu.make_async_copy(cols_ref, held.at[me], local_sem.at[0])
    own_rows = pltpu.make_async_copy(rows_ref, rows_vm, local_sem.at[1])
    own_cols.start()
    own_rows.start()

    barrier = pltpu.get_barrier_semaphore()

    for other in (after_me, before_me, sibling):
        pl.semaphore_signal(barrier, inc=1, device_id={"row": other}, device_id_type=MESH)
    recs[me, 0:1] = jnp.full((1, LANES), amp_ref[0], F32)
    recs[me, 1:2] = jnp.full((1, LANES), corr_ref[0], F32)
    noise_vm[...] = jnp.ones_like(noise_vm)
    noise_vm[:blocks, :] = noise_ref[...]
    pl.semaphore_wait(barrier, 3)

    def records(count):
        part = recs.at[pl.ds(0, count)]
        return pltpu.make_async_remote_copy(
            src_ref=part, dst_ref=part, send_sem=rec_send, recv_sem=rec_sib.at[0, m // 2],
            device_id={"row": sibling}, device_id_type=MESH,
        )

    def all_sent(count, sem):
        part = held.at[pl.ds(0, count)]
        pltpu.make_async_remote_copy(
            src_ref=part, dst_ref=part, send_sem=sem, recv_sem=sib_recv.at[0, steps],
            device_id={"row": sibling}, device_id_type=MESH,
        ).wait_send()

    def half_of(direction, h):
        return ((h + direction) % 2) * half

    def sign(direction):
        return 1 - 2 * direction

    def record_copy(direction, d, at):
        part = recs.at[device(at - sign(direction) * (d - 1), core)]
        return pltpu.make_async_remote_copy(
            src_ref=part, dst_ref=part, send_sem=rec_send, recv_sem=rec_recv.at[direction, d - 1],
            device_id={"row": after_me if direction == 0 else before_me}, device_id_type=MESH,
        )

    def record_sibling(direction, d, c):
        part = recs.at[device(pos - sign(direction) * d, c)]
        return pltpu.make_async_remote_copy(
            src_ref=part, dst_ref=part, send_sem=rec_send, recv_sem=rec_sib.at[direction, d - 1],
            device_id={"row": sibling}, device_id_type=MESH,
        )

    def record_own(c):
        part = recs.at[chip * 2 + c]
        return pltpu.make_async_remote_copy(
            src_ref=part, dst_ref=part, send_sem=rec_send, recv_sem=rec_sib.at[0, m // 2],
            device_id={"row": sibling}, device_id_type=MESH,
        )

    def ways(d):
        return 1 if isinstance(d, int) and d == m // 2 else 2

    def hop(d, more=None):
        for direction in range(ways(d)):
            record_copy(direction, d, pos - sign(direction)).wait_recv()
            if more or (more is None and d < m // 2 and direction < ways(d + 1)):
                record_copy(direction, d + 1, pos).start()
            record_sibling(direction, d, core).start()

    def ring_copy(direction, h, q, at, own=False):
        origin = device(at - sign(direction) * (h // 2), core)
        lines = pl.ds(half_of(direction, h) + q * (half // 2), half // 2)
        part = held.at[origin, lines]
        return pltpu.make_async_remote_copy(
            src_ref=cols_ref.at[lines] if own else part, dst_ref=part,
            send_sem=ring_send, recv_sem=ring_recv.at[direction, 2 * h + q],
            device_id={"row": after_me if direction == 0 else before_me}, device_id_type=MESH,
        )

    def sibling_copy(direction, h, c):
        origin = device(pos - sign(direction) * (h // 2 + 1), c)
        part = held.at[origin, pl.ds(half_of(direction, h), half)]
        return pltpu.make_async_remote_copy(
            src_ref=part, dst_ref=part,
            send_sem=sib_send, recv_sem=sib_recv.at[direction, h],
            device_id={"row": sibling}, device_id_type=MESH,
        )

    def own_copy(c):
        return pltpu.make_async_remote_copy(
            src_ref=cols_ref, dst_ref=held.at[chip * 2 + c],
            send_sem=sib_send, recv_sem=sib_recv.at[0, steps],
            device_id={"row": sibling}, device_id_type=MESH,
        )

    def send_own(h, q):
        for direction in range(2):
            ring_copy(direction, h, q, pos, True).start()

    for direction in range(2):
        record_copy(direction, 1, pos).start()
    record_own(core).start()
    send_own(0, 0)
    hop(1)
    for h, q in ((0, 1), (1, 0), (1, 1)):
        send_own(h, q)
    own_copy(core).start()

    def pass_on(h, q, more=None):
        more = h + 2 < steps if more is None else more
        for direction in range(2):
            ring_copy(direction, h, q, pos - sign(direction)).wait_recv()
            if more:
                ring_copy(direction, h + 2, q, pos).start()
            if q == 1:
                sibling_copy(direction, h, core).start()

    def take(k):
        for direction in range(2):
            sibling_copy(direction, k, 1 - core).wait_recv()

    def tiles(p):
        block = device(p, 0)
        pair = jnp.concatenate([held[block], held[block + 1]], axis=1)
        both = jnp.dot(lhs[...], pair, preferred_element_type=F32)
        both = both[:LANES] + both[LANES:]
        product[block] = both[:, :LANES]
        product[block + 1] = both[:, LANES:]

    own_rows.wait()
    for b in range(blocks):
        rows_t[:, b * LANES : (b + 1) * LANES] = (
            rows_vm[b * LANES : (b + 1) * LANES, :].astype(F32).T.astype(BF16)
        )
    u_ref[...] = jnp.zeros_like(u_ref)
    pass_on(0, 0)

    hop(2)
    pass_on(0, 1)
    hop(3)
    pass_on(1, 0)
    if m // 2 > 4:
        def hop_on(d, _):
            hop(d, True)
            return 0

        lax.fori_loop(4, m // 2 - 1, hop_on, 0)
        hop(m // 2 - 1)
    hop(m // 2)

    def take_record(d, _):
        for direction in range(2):
            record_sibling(direction, d, 1 - core).wait_recv()
        return 0

    lax.fori_loop(1, m // 2, take_record, 0)
    record_sibling(0, m // 2, 1 - core).wait_recv()
    record_own(1 - core).wait_recv()
    amp, corr, starts, place = record_terms(lengths_ref, record_ref, recs, noise_vm.shape)
    scale, log_g, gain = filter_terms(amp, corr, place, noise_vm[...])
    pass_on(1, 1)
    after, before = log_sums(log_g, place)
    cols = jnp.concatenate(
        [after, scale, starts, jnp.zeros((LANES - 3 * sub, LANES), F32)], axis=0
    ).T

    def mix(b):
        near = [b] if b == 0 else [b - 1, b]
        span = slice(near[0] * LANES, (b + 1) * LANES)
        wide = len(near) * LANES
        parts = [factor_block(b, other, cols, before, gain, starts) for other in near]
        both = jnp.concatenate([part[0] for part in parts] + [part[1] for part in parts], axis=1)
        left = rows_t[:, span]
        white = lax.dot_general(
            jnp.concatenate([left, left], axis=1), both, (((1,), (1,)), ((), ())), preferred_element_type=F32
        ).astype(BF16)
        back = jnp.dot(white, both, preferred_element_type=F32)
        u_ref[:, span] += back[:, :wide] + back[:, wide:]

    def tiles_at(d, direction):
        tiles(pos - sign(direction) * d)

    last = m // 2 - 1
    mix(0)
    mix(1)
    pass_on(2, 0)
    for b in range(2, blocks):
        mix(b)
    pass_on(2, 1)
    u = u_ref[...]
    high = u.astype(BF16)
    lhs[:LANES, :] = high
    lhs[LANES:, :] = (u - high.astype(F32)).astype(BF16)
    own_copy(1 - core).wait_recv()
    own_cols.wait()
    tiles(pos)
    pass_on(3, 0)
    take(0)
    take(1)
    tiles_at(1, 0)
    pass_on(3, 1)
    tiles_at(1, 1)

    def one(d, more):
        h = 2 * d - 2
        pass_on(h, 0, more)
        take(h - 2)
        take(h - 1)
        tiles_at(d - 1, 0)
        pass_on(h, 1, more)
        tiles_at(d - 1, 1)
        pass_on(h + 1, 0, more)
        pass_on(h + 1, 1, more)

    if last > 3:
        def body(d, _):
            one(d, True)
            return 0

        lax.fori_loop(3, last, body, 0)
    one(last, None)
    pass_on(steps - 1, 0)
    take(steps - 3)
    take(steps - 2)
    tiles_at(last, 0)
    pass_on(steps - 1, 1)
    tiles_at(last, 1)
    take(steps - 1)
    tiles(pos + m // 2)

    for j in range(n):
        out_ref[:, j * LANES : (j + 1) * LANES] = product[map_ref[j]]

    all_sent(m - 1, ring_send)
    all_sent(m, sib_send)
    records(n - 1).wait_send()


def gather_multiply(n, amp, corr, lengths, record, block_map, noise, rows, cols):
    obs, width = cols.shape
    sub = -(-noise.shape[0] // 8) * 8
    steps = n // 2 - 1
    smem = pl.BlockSpec(memory_space=pltpu.SMEM)
    vmem = pl.BlockSpec(memory_space=pltpu.VMEM)
    hbm = pl.BlockSpec(memory_space=pltpu.HBM)
    dma = pltpu.SemaphoreType.DMA
    return pl.pallas_call(
        functools.partial(kernel, n),
        out_shape=pltpu.VMEM((rows.shape[1], n * width), F32),
        in_specs=[smem, smem, smem, smem, smem, vmem, hbm, hbm],
        out_specs=vmem,
        scratch_shapes=[
            pltpu.VMEM((n, obs, width), BF16),
            pltpu.VMEM((n, LANES, width), F32),
            pltpu.VMEM((obs, LANES), BF16),
            pltpu.VMEM((LANES, obs), BF16),
            pltpu.VMEM((n, 8, LANES), F32),
            pltpu.VMEM((sub, LANES), F32),
            pltpu.VMEM((LANES, obs), F32),
            pltpu.VMEM((2 * LANES, obs), BF16),
            dma((2,)),
            dma,
            dma((2, n // 4)),
            dma((2, n // 4 + 1)),
            dma,
            dma((2, 2 * steps)),
            dma,
            dma((2, steps + 1)),
        ],
        compiler_params=pltpu.CompilerParams(
            collective_id=0, has_side_effects=True, vmem_limit_bytes=54 * 1024 * 1024
        ),
    )(amp, corr, lengths, record, block_map, noise, rows, cols)


def per_device(
    design_rows,
    design_cols,
    noise_std,
    record_noise_amplitude,
    record_correlation_length,
    arc_lengths,
    arc_record_index,
    block_map,
):
    n = lax.axis_size("row")
    noise = noise_std.reshape(-1, LANES)
    return gather_multiply(
        n,
        record_noise_amplitude,
        record_correlation_length,
        arc_lengths,
        arc_record_index,
        block_map,
        noise,
        design_rows,
        design_cols,
    )


def solution(mesh):
    return jax.shard_map(
        per_device,
        mesh=mesh,
        in_specs=(
            P("groups", "row"),
            P("groups", "row"),
            P("groups"),
            P(("groups", "row")),
            P(("groups", "row")),
            P("groups"),
            P("groups"),
            P("groups"),
        ),
        out_specs=P(("groups", "row"), None),
        check_vma=False,
    )
```

```python
import functools

import jax
import jax.numpy as jnp
from jax import lax
from jax.experimental import pallas as pl
from jax.experimental.pallas import tpu as pltpu
from jax.sharding import PartitionSpec as P

LANES = 128
MESH = pl.DeviceIdType.MESH
F32 = jnp.float32
BF16 = jnp.bfloat16


def flat_shift(x, d):
    rolled = pltpu.roll(x, d, 1)
    above = pltpu.roll(rolled, 1, 0)
    lane = lax.broadcasted_iota(jnp.int32, x.shape, 1)
    return jnp.where(lane < d, above, rolled)


def record_terms(lengths_ref, record_ref, recs, shape):
    flat = lax.broadcasted_iota(jnp.int32, shape, 0) * LANES + lax.broadcasted_iota(jnp.int32, shape, 1)
    start = jnp.int32(0)
    starts = jnp.zeros(shape, jnp.int32)
    amp = jnp.broadcast_to(recs[record_ref[0], 0:1], shape)
    corr = jnp.broadcast_to(recs[record_ref[0], 1:2], shape)
    for k in range(1, lengths_ref.shape[0]):
        start = start + lengths_ref[k - 1]
        here = flat >= start
        starts = jnp.where(here, start, starts)
        amp = jnp.where(here, recs[record_ref[k], 0:1], amp)
        corr = jnp.where(here, recs[record_ref[k], 1:2], corr)
    return amp, corr, starts.astype(F32), flat - starts


def filter_terms(amp, corr, place, noise):
    a2 = amp * amp
    phi = jnp.exp(-1.0 / corr)
    phi2 = phi * phi
    q = a2 * (1.0 - phi2)
    r = noise * noise
    rp = flat_shift(r, 1)
    first = place == 0
    m11 = jnp.where(first, 0.0, phi2 * rp + q)
    m12 = jnp.where(first, a2, q * rp)
    m21 = jnp.where(first, 0.0, 1.0)
    m22 = jnp.where(first, 1.0, rp)
    d = 1
    while d < LANES:
        n11, n12, n21, n22 = (flat_shift(x, d) for x in (m11, m12, m21, m22))
        p11 = m11 * n11 + m12 * n21
        p12 = m11 * n12 + m12 * n22
        p21 = m21 * n11 + m22 * n21
        p22 = m21 * n12 + m22 * n22
        m11, m12, m21, m22 = p11, p12, p21, p22
        if d in (4, 32):
            scale = 1.0 / (p11 + p12 + p21 + p22)
            m11, m12, m21, m22 = p11 * scale, p12 * scale, p21 * scale, p22 * scale
        d *= 2
    var = m12 / m22
    s = var + r
    inv_s = 1.0 / s
    return lax.rsqrt(s), jnp.log(phi * r * inv_s), phi * var * inv_s


def log_sums(log_g):
    high = log_g.astype(BF16).astype(F32)
    middle = (log_g - high).astype(BF16).astype(F32)
    terms = jnp.concatenate([high, middle, log_g - high - middle], axis=0).astype(BF16)
    i = lax.broadcasted_iota(jnp.int32, (LANES, LANES), 0)
    j = lax.broadcasted_iota(jnp.int32, (LANES, LANES), 1)
    ones = jnp.where(i <= j, 1.0, 0.0).astype(BF16)
    sums = jnp.dot(terms, ones, preferred_element_type=F32)
    sub = log_g.shape[0]
    total = sums[:sub] + sums[sub : 2 * sub] + sums[2 * sub :]
    return total - log_g, total, total - total[:, LANES - 1 :]


def factor_block(b, other, cols, before, before_next, gain, starts):
    sub = before.shape[0]
    a_i = cols[:, b : b + 1]
    s_i = cols[:, sub + b : sub + b + 1]
    t_i = cols[:, 2 * sub + b : 2 * sub + b + 1]
    value = -(s_i * gain[other : other + 1, :]) * jnp.exp(a_i - (before if other == b else before_next)[other : other + 1, :])
    live = t_i == starts[other : other + 1, :]
    if other == b:
        i = lax.broadcasted_iota(jnp.int32, (LANES, LANES), 0)
        j = lax.broadcasted_iota(jnp.int32, (LANES, LANES), 1)
        value = jnp.where(live & (j < i), value, jnp.where(i == j, s_i, 0.0))
    else:
        value = jnp.where(live, value, 0.0)
    high = value.astype(BF16)
    low = (value - high.astype(F32)).astype(BF16)
    return high, low


def kernel(
    n,
    amp_ref, corr_ref, lengths_ref, record_ref, map_ref, noise_ref, rows_ref, cols_ref,
    out_ref,
    held, product, rows_vm, rows_t, recs, noise_vm, u_ref, lhs,
    local_sem, rec_send, rec_recv, ring_send, ring_recv, sib_send, sib_recv,
):
    me = lax.axis_index("row")
    core = me % 2
    chip = me // 2
    sibling = chip * 2 + 1 - core
    m = n // 2
    pos = jnp.where(chip % 2 == 0, chip // 2, m - 1 - chip // 2)
    obs = rows_ref.shape[0]
    half = obs // 2
    blocks = obs // LANES
    steps = m - 1
    sub = noise_vm.shape[0]

    def device(p, c):
        p = (p + 2 * m) % m
        return jnp.where(p < m // 2, 2 * p, 2 * (m - 1 - p) + 1) * 2 + c

    after_me, before_me = device(pos + 1, core), device(pos - 1, core)
    own_cols = pltpu.make_async_copy(cols_ref, held.at[me], local_sem.at[0])
    own_rows = pltpu.make_async_copy(rows_ref, rows_vm, local_sem.at[1])
    own_cols.start()
    own_rows.start()

    barrier = pltpu.get_barrier_semaphore()

    def greet(o, _):
        pl.semaphore_signal(barrier, inc=1, device_id={"row": (me + o) % n}, device_id_type=MESH)
        return 0

    lax.fori_loop(1, n, greet, 0)
    recs[me, 0:1] = jnp.full((1, LANES), amp_ref[0], F32)
    recs[me, 1:2] = jnp.full((1, LANES), corr_ref[0], F32)
    noise_vm[...] = jnp.ones_like(noise_vm)
    noise_vm[:blocks, :] = noise_ref[...]
    pl.semaphore_wait(barrier, n - 1)

    def record_copy(source, target):
        return pltpu.make_async_remote_copy(
            src_ref=recs.at[source], dst_ref=recs.at[source],
            send_sem=rec_send, recv_sem=rec_recv,
            device_id={"row": target}, device_id_type=MESH,
        )

    def records(count):
        part = recs.at[pl.ds(0, count)]
        return pltpu.make_async_remote_copy(
            src_ref=part, dst_ref=part, send_sem=rec_send, recv_sem=rec_recv,
            device_id={"row": sibling}, device_id_type=MESH,
        )

    def all_sent(count, sem):
        part = held.at[pl.ds(0, count)]
        pltpu.make_async_remote_copy(
            src_ref=part, dst_ref=part, send_sem=sem, recv_sem=sib_recv.at[0, steps],
            device_id={"row": sibling}, device_id_type=MESH,
        ).wait_send()

    def send_record(o, _):
        record_copy(me, (me + o) % n).start()
        return 0

    def half_of(direction, h):
        return ((h + direction) % 2) * half

    def sign(direction):
        return 1 - 2 * direction

    def ring_copy(direction, h, q, at, own=False):
        origin = device(at - sign(direction) * (h // 2), core)
        lines = pl.ds(half_of(direction, h) + q * (half // 2), half // 2)
        part = held.at[origin, lines]
        return pltpu.make_async_remote_copy(
            src_ref=cols_ref.at[lines] if own else part, dst_ref=part,
            send_sem=ring_send, recv_sem=ring_recv.at[direction, 2 * h + q],
            device_id={"row": after_me if direction == 0 else before_me}, device_id_type=MESH,
        )

    def sibling_copy(direction, h, c):
        origin = device(pos - sign(direction) * (h // 2 + 1), c)
        part = held.at[origin, pl.ds(half_of(direction, h), half)]
        return pltpu.make_async_remote_copy(
            src_ref=part, dst_ref=part,
            send_sem=sib_send, recv_sem=sib_recv.at[direction, h],
            device_id={"row": sibling}, device_id_type=MESH,
        )

    def own_copy(c):
        return pltpu.make_async_remote_copy(
            src_ref=cols_ref, dst_ref=held.at[chip * 2 + c],
            send_sem=sib_send, recv_sem=sib_recv.at[0, steps],
            device_id={"row": sibling}, device_id_type=MESH,
        )

    lax.fori_loop(1, n, send_record, 0)
    for h, q in ((0, 0), (0, 1), (1, 0), (1, 1)):
        for direction in range(2):
            ring_copy(direction, h, q, pos, True).start()
    own_copy(core).start()

    def pass_on(h, q, more=None):
        more = h + 2 < steps if more is None else more
        for direction in range(2):
            ring_copy(direction, h, q, pos - sign(direction)).wait_recv()
            if more:
                ring_copy(direction, h + 2, q, pos).start()
            if q == 1:
                sibling_copy(direction, h, core).start()

    def take(k):
        for direction in range(2):
            sibling_copy(direction, k, 1 - core).wait_recv()

    def tiles(p):
        block = device(p, 0)
        pair = jnp.concatenate([held[block], held[block + 1]], axis=1)
        both = jnp.dot(lhs[...], pair, preferred_element_type=F32)
        both = both[:LANES] + both[LANES:]
        product[block] = both[:, :LANES]
        product[block + 1] = both[:, LANES:]

    own_rows.wait()
    for b in range(blocks):
        rows_t[:, b * LANES : (b + 1) * LANES] = (
            rows_vm[b * LANES : (b + 1) * LANES, :].astype(F32).T.astype(BF16)
        )
    u_ref[...] = jnp.zeros_like(u_ref)

    records(n - 1).wait_recv()
    amp, corr, starts, place = record_terms(lengths_ref, record_ref, recs, noise_vm.shape)
    scale, log_g, gain = filter_terms(amp, corr, place, noise_vm[...])
    pass_on(0, 0)
    pass_on(0, 1)
    after, before, before_next = log_sums(log_g)
    cols = jnp.concatenate(
        [after, scale, starts, jnp.zeros((LANES - 3 * sub, LANES), F32)], axis=0
    ).T

    def mix(b):
        near = [b] if b == 0 else [b - 1, b]
        span = slice(near[0] * LANES, (b + 1) * LANES)
        wide = len(near) * LANES
        parts = [factor_block(b, other, cols, before, before_next, gain, starts) for other in near]
        both = jnp.concatenate([part[0] for part in parts] + [part[1] for part in parts], axis=1)
        left = rows_t[:, span]
        white = lax.dot_general(
            jnp.concatenate([left, left], axis=1), both, (((1,), (1,)), ((), ())), preferred_element_type=F32
        ).astype(BF16)
        back = jnp.dot(white, both, preferred_element_type=F32)
        u_ref[:, span] += back[:, :wide] + back[:, wide:]

    def tiles_at(d, direction):
        tiles(pos - sign(direction) * d)

    last = m // 2 - 1
    pass_on(1, 0)
    mix(0)
    mix(1)
    pass_on(1, 1)
    mix(2)
    mix(3)
    pass_on(2, 0)
    for b in range(4, blocks):
        mix(b)
    pass_on(2, 1)
    u = u_ref[...]
    high = u.astype(BF16)
    lhs[:LANES, :] = high
    lhs[LANES:, :] = (u - high.astype(F32)).astype(BF16)
    own_copy(1 - core).wait_recv()
    own_cols.wait()
    tiles(pos)
    pass_on(3, 0)
    take(0)
    take(1)
    tiles_at(1, 0)
    pass_on(3, 1)
    tiles_at(1, 1)

    def one(d, more):
        h = 2 * d - 2
        pass_on(h, 0, more)
        take(h - 2)
        take(h - 1)
        tiles_at(d - 1, 0)
        pass_on(h, 1, more)
        tiles_at(d - 1, 1)
        pass_on(h + 1, 0, more)
        pass_on(h + 1, 1, more)

    if last > 3:
        def body(d, _):
            one(d, True)
            return 0

        lax.fori_loop(3, last, body, 0)
    one(last, None)
    pass_on(steps - 1, 0)
    take(steps - 3)
    take(steps - 2)
    tiles_at(last, 0)
    pass_on(steps - 1, 1)
    tiles_at(last, 1)
    take(steps - 1)
    tiles(pos + m // 2)

    for j in range(n):
        out_ref[:, j * LANES : (j + 1) * LANES] = product[map_ref[j]]

    all_sent(m - 1, ring_send)
    all_sent(m, sib_send)
    records(n - 1).wait_send()


def gather_multiply(n, amp, corr, lengths, record, block_map, noise, rows, cols):
    obs, width = cols.shape
    sub = -(-noise.shape[0] // 8) * 8
    steps = n // 2 - 1
    smem = pl.BlockSpec(memory_space=pltpu.SMEM)
    vmem = pl.BlockSpec(memory_space=pltpu.VMEM)
    hbm = pl.BlockSpec(memory_space=pltpu.HBM)
    dma = pltpu.SemaphoreType.DMA
    return pl.pallas_call(
        functools.partial(kernel, n),
        out_shape=pltpu.VMEM((rows.shape[1], n * width), F32),
        in_specs=[smem, smem, smem, smem, smem, vmem, hbm, hbm],
        out_specs=vmem,
        scratch_shapes=[
            pltpu.VMEM((n, obs, width), BF16),
            pltpu.VMEM((n, LANES, width), F32),
            pltpu.VMEM((obs, LANES), BF16),
            pltpu.VMEM((LANES, obs), BF16),
            pltpu.VMEM((n, 8, LANES), F32),
            pltpu.VMEM((sub, LANES), F32),
            pltpu.VMEM((LANES, obs), F32),
            pltpu.VMEM((2 * LANES, obs), BF16),
            dma((2,)),
            dma,
            dma,
            dma,
            dma((2, 2 * steps)),
            dma,
            dma((2, steps + 1)),
        ],
        compiler_params=pltpu.CompilerParams(
            collective_id=0, has_side_effects=True, vmem_limit_bytes=54 * 1024 * 1024
        ),
    )(amp, corr, lengths, record, block_map, noise, rows, cols)


def per_device(
    design_rows,
    design_cols,
    noise_std,
    record_noise_amplitude,
    record_correlation_length,
    arc_lengths,
    arc_record_index,
    block_map,
):
    n = lax.axis_size("row")
    noise = noise_std.reshape(-1, LANES)
    return gather_multiply(
        n,
        record_noise_amplitude,
        record_correlation_length,
        arc_lengths,
        arc_record_index,
        block_map,
        noise,
        design_rows,
        design_cols,
    )


def solution(mesh):
    return jax.shard_map(
        per_device,
        mesh=mesh,
        in_specs=(
            P("groups", "row"),
            P("groups", "row"),
            P("groups"),
            P(("groups", "row")),
            P(("groups", "row")),
            P("groups"),
            P("groups"),
            P("groups"),
        ),
        out_specs=P(("groups", "row"), None),
        check_vma=False,
    )
```
